256 devices in a mesh: frames: 64 (over y, z, x_hi), band: 4 (over x_lo, core).
Axes of the slice: x: 4 (x_hi: 2, x_lo: 2; x = x_hi * 2 + x_lo), y: 4, z: 8, core: 2. Of those that a mesh axis runs over, the one named last changes fastest.
Arguments:
- tokens: bfloat16 [128, 1024, 1024], P('frames', 'band'), may hold values from -6 to 6
- norm_space: float32 [1024], replicated, may hold values from 0.5 to 1.5
- query_space: bfloat16 [1024, 1024], replicated, may hold values from -0.1875 to 0.1875
- keyval_space: bfloat16 [1024, 512], replicated, may hold values from -0.1875 to 0.1875
- out_space: bfloat16 [1024, 1024], replicated, may hold values from -0.1875 to 0.1875
- qk_space: float32 [2, 64], replicated, may hold values from 0.7 to 7
- norm_time: float32 [1024], replicated, may hold values from 0.5 to 1.5
- query_time: bfloat16 [1024, 1024], replicated, may hold values from -0.1875 to 0.1875
- keyval_time: bfloat16 [1024, 512], replicated, may hold values from -0.1875 to 0.1875
- out_time: bfloat16 [1024, 1024], replicated, may hold values from -0.1875 to 0.1875
- qk_time: float32 [2, 64], replicated, may hold values from 0.7 to 7
Outputs:
- mixed: bfloat16 [128, 1024, 1024], P('frames', 'band')
The draws below stay inside these ranges and needn't reach their ends.
All inputs are finite; a program needn't handle non-finite values.
Results may differ from the reference program's by a relative error of at most 0.025.
The reference program's roundings to bfloat16 on the way count: a program that leaves them out, or rounds other values in their place, can miss the bound.
Values may be sent and summed in bfloat16 or wider, within the bound.
A program may use at most 128 MiB of HBM per device.

```python
import jax
import jax.numpy as jnp
from jax import lax

D = 1024
HEADS = 16
KV_HEADS = 4
HEAD_DIM = 64
PATCHES = 1024
FRAMES = 128


def draw_qk_space(key, part):
    sub_key = jax.random.fold_in(key, 11)
    return jax.random.uniform(sub_key, (2, HEAD_DIM), jnp.float32, 0.7, 1.4)


def draw_qk_time(key, part):
    sub_key = jax.random.fold_in(key, 23)
    return jax.random.uniform(sub_key, (2, HEAD_DIM), jnp.float32, 0.7, 1.4)


def steps_of(stream_key, shape, split, low, high):
    def one(dim, shards_of):
        draws = jax.random.uniform(jax.random.fold_in(jax.random.fold_in(stream_key, 6), dim), (shards_of,), jnp.float32, low / len(split), high / len(split))
        return jnp.repeat(jnp.exp(draws), shape[dim] // shards_of).reshape((-1,) + (1,) * (len(shape) - dim - 1))

    loudness = one(*split[0])
    for cut in split[1:]:
        loudness = loudness * one(*cut)
    return loudness


def noise(stream_key, extent, deviation, most, cuts=(), kind=jnp.bfloat16):
    result = deviation * jax.random.normal(stream_key, extent, jnp.float32)
    if cuts:
        result = result * steps_of(stream_key, extent, cuts, -0.22, 0.18)
    return jnp.clip(result, -most, most).astype(kind)


def setup_inputs(seed: int = 0) -> dict:
    key_list = jax.random.split(jax.random.key(seed), 12)
    tokens = noise(key_list[0], (FRAMES, PATCHES, D), 1.0, 6.0, ((0, 64), (1, 4)))
    norm_space = jnp.clip(jax.random.uniform(key_list[1], (D,), jnp.float32, 0.5, 1.5), 0.5, 1.5)
    query_space = noise(key_list[2], (D, HEADS * HEAD_DIM), D ** -0.5, 0.1875)
    keyval_space = noise(key_list[3], (D, 2 * KV_HEADS * HEAD_DIM), D ** -0.5, 0.1875)
    out_space = noise(key_list[4], (HEADS * HEAD_DIM, D), (HEADS * HEAD_DIM) ** -0.5, 0.1875)
    qk_space = draw_qk_space(jax.random.fold_in(key_list[11], 71), 0)
    norm_time = jnp.clip(jax.random.uniform(key_list[6], (D,), jnp.float32, 0.5, 1.5), 0.5, 1.5)
    query_time = noise(key_list[7], (D, HEADS * HEAD_DIM), D ** -0.5, 0.1875)
    keyval_time = noise(key_list[8], (D, 2 * KV_HEADS * HEAD_DIM), D ** -0.5, 0.1875)
    out_time = noise(key_list[9], (HEADS * HEAD_DIM, D), (HEADS * HEAD_DIM) ** -0.5, 0.1875)
    qk_time = draw_qk_time(jax.random.fold_in(key_list[11], 71), 0)
    return dict(tokens=tokens, norm_space=norm_space, query_space=query_space, keyval_space=keyval_space, out_space=out_space, qk_space=qk_space, norm_time=norm_time, query_time=query_time, keyval_time=keyval_time, out_time=out_time, qk_time=qk_time)


def rms_rows(values, gain):
    values = values.astype(jnp.float32)
    scaled = lax.rsqrt(lax.optimization_barrier(jnp.mean(values * values, axis=-1, keepdims=True)) + 1e-06)
    return values * scaled * gain

def project(hidden, w_query, w_keyval, qk_gain):
    row_count = hidden.shape[0]
    queries = jnp.dot(hidden, w_query, preferred_element_type=jnp.float32)
    keyval = jnp.dot(hidden, w_keyval, preferred_element_type=jnp.float32)
    queries = rms_rows(queries.reshape(row_count, HEADS, HEAD_DIM), qk_gain[0])
    key_part = keyval[:, :KV_HEADS * HEAD_DIM].reshape(row_count, KV_HEADS, HEAD_DIM)
    key_rows = rms_rows(key_part, qk_gain[1])
    values = keyval[:, KV_HEADS * HEAD_DIM:]
    return (queries.reshape(row_count, -1).astype(jnp.bfloat16), key_rows.reshape(row_count, -1).astype(jnp.bfloat16), values.astype(jnp.bfloat16))

def attend(queries, key_rows, values, causal_mask):
    query_count = queries.shape[0]
    key_count = key_rows.shape[0]
    groups = HEADS // KV_HEADS
    grouped = queries.astype(jnp.float32).reshape(query_count, KV_HEADS, groups, HEAD_DIM)
    key_heads = key_rows.astype(jnp.float32).reshape(key_count, KV_HEADS, HEAD_DIM)
    value_heads = values.astype(jnp.float32).reshape(key_count, KV_HEADS, HEAD_DIM)
    scores = jnp.einsum('nkgd,mkd->kgnm', grouped, key_heads) * HEAD_DIM ** (-0.5)
    if causal_mask is not None:
        scores = jnp.where(causal_mask, scores, -jnp.inf)
    largest = lax.optimization_barrier(jnp.max(scores, axis=-1, keepdims=True))
    expos = jnp.exp(scores - largest)
    totals = lax.optimization_barrier(jnp.sum(expos, axis=-1))
    weights = expos.astype(jnp.bfloat16).astype(jnp.float32)
    summed = jnp.einsum('kgnm,mkd->nkgd', weights, value_heads)
    summed = summed / jnp.transpose(totals, (2, 0, 1))[..., None]
    return summed.reshape(query_count, HEADS * HEAD_DIM).astype(jnp.bfloat16)

def reference(tokens, norm_space, query_space, keyval_space, out_space, qk_space, norm_time, query_time, keyval_time, out_time, qk_time):

    def space_frame(frame_tokens):
        normed = rms_rows(frame_tokens, norm_space).astype(jnp.bfloat16)
        queries, key_rows, values = project(normed, query_space, keyval_space, qk_space)
        attended = attend(queries, key_rows, values, None)
        update = jnp.dot(attended, out_space, preferred_element_type=jnp.float32)
        stream = (frame_tokens.astype(jnp.float32) + update).astype(jnp.bfloat16)
        normed_time = rms_rows(stream, norm_time).astype(jnp.bfloat16)
        time_q, time_k, time_v = project(normed_time, query_time, keyval_time, qk_time)
        return (stream, time_q, time_k, time_v)
    stream, time_q, time_k, time_v = lax.map(space_frame, tokens)
    frame_count = tokens.shape[0]
    order = jnp.arange(frame_count, dtype=jnp.int32)
    causal_mask = order[:, None] >= order[None, :]
    block_rows = 256

    def regroup(array):
        moved = jnp.swapaxes(array, 0, 1)
        return moved.reshape(PATCHES // block_rows, block_rows, frame_count, array.shape[-1])

    def time_block(pieces):
        block_q, block_k, block_v = pieces
        return jax.vmap(lambda qq, kk, vv: attend(qq, kk, vv, causal_mask))(block_q, block_k, block_v)
    attended = lax.map(time_block, (regroup(time_q), regroup(time_k), regroup(time_v)))
    attended = jnp.swapaxes(attended.reshape(PATCHES, frame_count, HEADS * HEAD_DIM), 0, 1)

    def out_frame(pieces):
        frame_stream, frame_att = pieces
        update = jnp.dot(frame_att, out_time, preferred_element_type=jnp.float32)
        return (frame_stream.astype(jnp.float32) + update).astype(jnp.bfloat16)
    return lax.map(out_frame, (stream, attended))
```

```python
import functools

import jax
import jax.numpy as jnp
from jax import lax
from jax.experimental import pallas as pl
from jax.experimental.pallas import tpu as pltpu
from jax.sharding import PartitionSpec as P

HEADS = 16
KV_HEADS = 4
HEAD_DIM = 64
D = 1024
ROWS = 256
PEERS = 64
POS = 4
MESH = pl.DeviceIdType.MESH
F32 = jnp.float32
BF16 = jnp.bfloat16
EXP_SCALE = 0.125 * 1.4426950408889634


def lane_half(shape):
    return lax.broadcasted_iota(jnp.int32, shape, len(shape) - 1) // HEAD_DIM


def rms_pair(tile, gain, ones_block):
    squares = tile * tile
    high = squares.astype(BF16)
    low = (squares - high.astype(F32)).astype(BF16)
    mean = jnp.dot(jnp.concatenate([high, low], axis=1), ones_block, preferred_element_type=F32)
    return tile * lax.rsqrt(mean + 1e-06) * gain


def head_queries(tile, pair):
    parity = (pair // 2) % 2
    here = lane_half(tile.shape) == parity
    turned = pltpu.roll(tile, HEAD_DIM, 1)
    first, second = (tile, turned) if parity == 0 else (turned, tile)
    zero = jnp.zeros_like(tile)
    return jnp.where(here, first, zero).astype(BF16), jnp.where(here, second, zero).astype(BF16)


def join_heads(first, second, parity):
    first = first * (1.0 / pltpu.roll(first, HEAD_DIM, 1))
    second = second * (1.0 / pltpu.roll(second, HEAD_DIM, 1))
    low = lane_half(first.shape) == 0
    if parity == 0:
        return jnp.where(low, first, pltpu.roll(second, HEAD_DIM, 1))
    return jnp.where(low, pltpu.roll(first, HEAD_DIM, 1), second)


def with_ones(tile, parity):
    return jnp.where(lane_half(tile.shape) == parity, tile, jnp.ones_like(tile))


def pack_rows(left, right):
    left = left.reshape(32, 8, 128)
    right = right.reshape(32, 8, 128)
    low = lax.broadcasted_iota(jnp.int32, left.shape, 1) < 4
    even = jnp.where(low, left, pltpu.roll(right, 4, 1))
    odd = jnp.where(low, pltpu.roll(left, 4, 1), right)
    return jnp.stack([even, odd], axis=1).reshape(PEERS, 8, 128)


def unpack_rows(packed):
    packed = packed.reshape(32, 2, 8, 128)
    even, odd = packed[:, 0], packed[:, 1]
    low = lax.broadcasted_iota(jnp.int32, even.shape, 1) < 4
    left = jnp.where(low, even, pltpu.roll(odd, 4, 1))
    right = jnp.where(low, pltpu.roll(even, 4, 1), odd)
    return left.reshape(ROWS, 128), right.reshape(ROWS, 128)


def gain_row(ref):
    return jnp.concatenate([ref[k : k + 1, :] for k in range(8)], axis=1)


def normalise(values, gain):
    return (values * lax.rsqrt(jnp.mean(values * values, axis=-1, keepdims=True) + 1e-06) * gain).astype(BF16)


def kernel(
    tok_hbm, ns_ref, wqs_hbm, wkvs_hbm, wos_hbm, qks_ref, nt_ref, wqt_hbm, wkvt_hbm, wot_hbm, qkt_ref,
    out_hbm,
    tok, wqs, wkvs, wos, wqt, wkvt, wot,
    normed, queries, kv_all, keys_t, vals, att, send_buf, recv_buf,
    shuffle, stream_t, normed_t, queries_t, keys_time, vals_time, att_t, back_buf, home_buf, out_buf,
    load_sem, kv_send, kv_recv, a2a_send, a2a_recv, back_send, back_recv, out_sem,
):
    me = lax.axis_index("frames")
    band = lax.axis_index("band")
    core_peer = lax.bitwise_xor(band, 1)
    chip_peer = lax.bitwise_xor(band, 2)

    loads = {}
    for k, (name, src, dst) in enumerate(
        [("tok", tok_hbm, tok), ("wkvs", wkvs_hbm, wkvs), ("wqs", wqs_hbm, wqs), ("wos", wos_hbm, wos),
         ("wqt", wqt_hbm, wqt), ("wkvt", wkvt_hbm, wkvt), ("wot", wot_hbm, wot)]
    ):
        loads[name] = pltpu.make_async_copy(src, dst, load_sem.at[k])
        loads[name].start()

    barrier = pltpu.get_barrier_semaphore()

    def greet(k, carry):
        pl.semaphore_signal(barrier, inc=1, device_id={"frames": lax.rem(me + k, PEERS)}, device_id_type=MESH)
        return carry

    lax.fori_loop(1, PEERS, greet, 0)
    for peer in (core_peer, chip_peer):
        pl.semaphore_signal(barrier, inc=1, device_id={"band": peer}, device_id_type=MESH)

    row = lax.broadcasted_iota(jnp.int32, (256, 128), 0)
    col = lax.broadcasted_iota(jnp.int32, (256, 128), 1)
    ones_block = jnp.where((row // HEAD_DIM) % 2 == col // HEAD_DIM, 1.0 / HEAD_DIM, 0.0).astype(BF16)

    def pair_gain(ref, k):
        return jnp.concatenate([ref[k : k + 1, :], ref[k : k + 1, :]], axis=1)

    loads["tok"].wait()
    gain_space = gain_row(ns_ref)

    def norm_rows(k, carry):
        rows = pl.ds(pl.multiple_of(k * 64, 64), 64)
        normed[rows, :] = normalise(tok[rows, :].astype(F32), gain_space)
        return carry

    lax.fori_loop(0, 2 * ROWS // 64, norm_rows, 0)

    def kv_copy(frame, slot, kind, peer):
        return pltpu.make_async_remote_copy(
            src_ref=kv_all.at[frame, slot], dst_ref=kv_all.at[frame, slot],
            send_sem=kv_send.at[frame, kind], recv_sem=kv_recv.at[frame, kind],
            device_id={"band": peer}, device_id_type=MESH)

    loads["wkvs"].wait()
    key_gain = pair_gain(qks_ref, 1)
    for frame in range(2):
        rows = slice(frame * ROWS, (frame + 1) * ROWS)
        part = jnp.dot(normed[rows, :], wkvs[...], preferred_element_type=F32)
        for t in range(2):
            tile = part[:, t * 128 : (t + 1) * 128]
            kv_all[frame, band, :, t * 128 : (t + 1) * 128] = rms_pair(tile, key_gain, ones_block).astype(BF16)
        kv_all[frame, band, :, 256:512] = part[:, 256:].astype(BF16)
        if frame == 0:
            pl.semaphore_wait(barrier, PEERS - 1 + 2)
        kv_copy(frame, band, 1, chip_peer).start()
        kv_copy(frame, band, 0, core_peer).start()

    loads["wqs"].wait()
    query_gain = pair_gain(qks_ref, 0)
    for n in range(4):
        part = jnp.dot(normed[...], wqs[:, n * 256 : (n + 1) * 256], preferred_element_type=F32)
        for k in range(2):
            pair = 2 * n + k
            tile = rms_pair(part[:, k * 128 : (k + 1) * 128], query_gain, ones_block)
            first, second = head_queries(tile, pair)
            queries[2 * pair] = first
            queries[2 * pair + 1] = second

    def forward(frame):
        kv_copy(frame, chip_peer, 1, chip_peer).wait_recv()
        kv_copy(frame, chip_peer, 2, core_peer).start()

    def space_frame(frame):
        kv_copy(frame, core_peer, 0, core_peer).wait_recv()
        kv_copy(frame, lax.bitwise_xor(band, 3), 2, core_peer).wait_recv()
        for src in range(4):
            at = slice(src * ROWS, (src + 1) * ROWS)
            for t in range(2):
                keys_t[t, :, at] = kv_all[frame, src, :, t * 128 : (t + 1) * 128].T
                value_tile = kv_all[frame, src, :, 256 + t * 128 : 256 + (t + 1) * 128]
                for parity in range(2):
                    vals[2 * t + parity, at, :] = with_ones(value_tile, parity)

        def one_kv(t, carry):
            for parity in range(2):
                for k in range(2):
                    pair = 4 * t + 2 * parity + k
                    done = []
                    for h in range(2):
                        q = queries[2 * pair + h, frame * ROWS : (frame + 1) * ROWS, :]
                        scores = jnp.dot(q, keys_t[t], preferred_element_type=F32)
                        largest = jnp.max(scores, axis=-1, keepdims=True)
                        weights = jnp.exp2((scores - largest) * EXP_SCALE).astype(BF16)
                        done.append(jnp.dot(weights, vals[2 * t + parity], preferred_element_type=F32))
                    att[pair] = join_heads(done[0], done[1], parity).astype(BF16)
            return carry

        lax.fori_loop(0, 2, one_kv, 0)

    def block_columns(left_ref, w_ref, n):
        left = jnp.concatenate([left_ref[k] for k in range(8)], axis=1)
        return jnp.dot(left, w_ref[:, n * 256 : (n + 1) * 256], preferred_element_type=F32)

    def send_all(buf, dst, frame, send_sem, recv_sem):
        def send(k, carry):
            peer = lax.rem(me + k, PEERS)
            pltpu.make_async_remote_copy(
                src_ref=buf.at[frame, peer], dst_ref=dst.at[frame, me],
                send_sem=send_sem.at[frame], recv_sem=recv_sem.at[frame],
                device_id={"frames": peer}, device_id_type=MESH).start()
            return carry

        lax.fori_loop(1, PEERS, send, 0)
        dst[frame, me] = buf[frame, me]

    def all_of(buf, dst, frame, send_sem, recv_sem):
        return pltpu.make_async_remote_copy(
            src_ref=buf.at[frame, pl.ds(0, PEERS - 1)], dst_ref=dst.at[frame, pl.ds(0, PEERS - 1)],
            send_sem=send_sem.at[frame], recv_sem=recv_sem.at[frame],
            device_id={"frames": me}, device_id_type=MESH)

    def out_space(frame):
        rows = slice(frame * ROWS, (frame + 1) * ROWS)
        for n in range(2):
            packs = []
            for m in (n, n + 2):
                at = slice(m * 256, (m + 1) * 256)
                stream = tok[rows, at].astype(F32) + block_columns(att, wos, m)
                stream = stream.astype(BF16).astype(F32)
                packs.append(pack_rows(stream[:, :128], stream[:, 128:]))
            send_buf[frame, :, :, n * 128 : (n + 1) * 128] = jnp.concatenate(packs, axis=1).astype(BF16)
        send_all(send_buf, recv_buf, frame, a2a_send, a2a_recv)

    forward(0)
    space_frame(0)
    forward(1)
    loads["wos"].wait()
    out_space(0)
    space_frame(1)
    out_space(1)

    gain_time = gain_row(nt_ref)
    query_gain_t = pair_gain(qkt_ref, 0)
    key_gain_t = pair_gain(qkt_ref, 1)
    for name in ("wqt", "wkvt", "wot"):
        loads[name].wait()

    def arrive(frame):
        all_of(send_buf, recv_buf, frame, a2a_send, a2a_recv).wait_recv()
        for n in range(2):
            pack = recv_buf[frame, :, :, n * 128 : (n + 1) * 128].astype(F32)
            for half, m in enumerate((n, n + 2)):
                left, right = unpack_rows(pack[:, half * 8 : (half + 1) * 8, :])
                shuffle[2 * m] = left
                shuffle[2 * m + 1] = right
        for j in range(POS):
            rows = slice(j * 64, (j + 1) * 64)
            values = jnp.concatenate([shuffle[k, pl.ds(j, 64, stride=4), :] for k in range(8)], axis=1)
            stream_t[frame, rows, :] = values.astype(BF16)
            normed_t[rows, :] = normalise(values, gain_time)
        hidden = normed_t[...]
        part = jnp.dot(hidden, wkvt[...], preferred_element_type=F32)
        keep = slice(frame * 64, (frame + 1) * 64)
        for t in range(2):
            tile = rms_pair(part[:, t * 128 : (t + 1) * 128], key_gain_t, ones_block).astype(BF16)
            value_tile = part[:, 256 + t * 128 : 256 + (t + 1) * 128].astype(BF16)
            for j in range(POS):
                rows = slice(j * 64, (j + 1) * 64)
                keys_time[j, t, keep, :] = tile[rows]
                for parity in range(2):
                    vals_time[j, 2 * t + parity, keep, :] = with_ones(value_tile[rows], parity)
        for n in range(4):
            part = jnp.dot(hidden, wqt[:, n * 256 : (n + 1) * 256], preferred_element_type=F32)
            for k in range(2):
                pair = 2 * n + k
                tile = rms_pair(part[:, k * 128 : (k + 1) * 128], query_gain_t, ones_block)
                first, second = head_queries(tile, pair)
                for j in range(POS):
                    rows = slice(j * 64, (j + 1) * 64)
                    queries_t[frame, j, 2 * pair] = first[rows]
                    queries_t[frame, j, 2 * pair + 1] = second[rows]

    def time_half(frame):
        q_frame = 2 * lax.broadcasted_iota(jnp.int32, (64, 128), 0) + frame
        k_row = lax.broadcasted_iota(jnp.int32, (64, 128), 1)
        allowed = q_frame >= 2 * (k_row % 64) + k_row // 64

        def position(j, carry):
            rows = pl.ds(pl.multiple_of(j * 64, 64), 64)
            for t in range(2):
                q = queries_t[frame, j, 8 * t : 8 * (t + 1)].reshape(512, 128)
                scores = lax.dot_general(q, keys_time[j, t], (((1,), (1,)), ((), ())), preferred_element_type=F32)
                scores = jnp.where(allowed[None], scores.reshape(8, 64, 128), -1e30)
                largest = jnp.max(scores, axis=-1, keepdims=True)
                weights = jnp.exp2((scores - largest) * EXP_SCALE).astype(BF16)
                for parity in range(2):
                    mine = weights[4 * parity : 4 * parity + 4].reshape(256, 128)
                    done = jnp.dot(mine, vals_time[j, 2 * t + parity], preferred_element_type=F32)
                    for k in range(2):
                        pair = 4 * t + 2 * parity + k
                        att_t[pair, rows, :] = join_heads(
                            done[k * 128 : k * 128 + 64], done[k * 128 + 64 : k * 128 + 128], parity
                        ).astype(BF16)
            return carry

        lax.fori_loop(0, POS, position, 0)
        for n in range(4):
            at = slice(n * 256, (n + 1) * 256)
            mixed = stream_t[frame, :, at].astype(F32) + block_columns(att_t, wot, n)
            mixed = mixed.astype(BF16).astype(F32)
            for j in range(POS):
                for half in range(2):
                    shuffle[2 * n + half, pl.ds(j, 64, stride=4), :] = mixed[
                        j * 64 : (j + 1) * 64, half * 128 : (half + 1) * 128]
        for n in range(2):
            packs = [pack_rows(shuffle[2 * m], shuffle[2 * m + 1]) for m in (n, n + 2)]
            back_buf[frame, :, :, n * 128 : (n + 1) * 128] = jnp.concatenate(packs, axis=1).astype(BF16)
        send_all(back_buf, home_buf, frame, back_send, back_recv)

    arrive(0)
    arrive(1)
    time_half(0)
    time_half(1)

    def finish(frame):
        all_of(back_buf, home_buf, frame, back_send, back_recv).wait_recv()
        for n in range(2):
            pack = home_buf[frame, :, :, n * 128 : (n + 1) * 128].astype(F32)
            for half, m in enumerate((n, n + 2)):
                left, right = unpack_rows(pack[:, half * 8 : (half + 1) * 8, :])
                out_buf[frame, :, m * 256 : m * 256 + 128] = left.astype(BF16)
                out_buf[frame, :, m * 256 + 128 : (m + 1) * 256] = right.astype(BF16)
        copy = pltpu.make_async_copy(out_buf.at[frame], out_hbm.at[frame], out_sem.at[frame])
        copy.start()
        return copy

    copies = [finish(0), finish(1)]
    for frame in range(2):
        kv_copy(frame, band, 0, core_peer).wait_send()
        kv_copy(frame, band, 1, chip_peer).wait_send()
        kv_copy(frame, chip_peer, 2, core_peer).wait_send()
        all_of(send_buf, recv_buf, frame, a2a_send, a2a_recv).wait_send()
        all_of(back_buf, home_buf, frame, back_send, back_recv).wait_send()
        copies[frame].wait()


def body(tokens, norm_space, query_space, keyval_space, out_space, qk_space,
         norm_time, query_time, keyval_time, out_time, qk_time):
    frames_here, rows_here, width = tokens.shape
    any_spec = pl.BlockSpec(memory_space=pl.ANY)
    vmem = pl.BlockSpec(memory_space=pltpu.VMEM)
    dma = pltpu.SemaphoreType.DMA
    return pl.pallas_call(
        kernel,
        out_shape=jax.ShapeDtypeStruct((frames_here, rows_here, width), BF16),
        in_specs=[any_spec, vmem, any_spec, any_spec, any_spec, vmem, vmem, any_spec, any_spec, any_spec, vmem],
        out_specs=any_spec,
        scratch_shapes=[
            pltpu.VMEM((2 * ROWS, D), BF16),
            pltpu.VMEM((D, D), BF16), pltpu.VMEM((D, 512), BF16), pltpu.VMEM((D, D), BF16),
            pltpu.VMEM((D, D), BF16), pltpu.VMEM((D, 512), BF16), pltpu.VMEM((D, D), BF16),
            pltpu.VMEM((2 * ROWS, D), BF16),
            pltpu.VMEM((HEADS, 2 * ROWS, 128), BF16),
            pltpu.VMEM((2, 4, ROWS, 512), BF16),
            pltpu.VMEM((2, 128, 4 * ROWS), BF16),
            pltpu.VMEM((KV_HEADS, 4 * ROWS, 128), BF16),
            pltpu.VMEM((8, ROWS, 128), BF16),
            pltpu.VMEM((2, PEERS, 16, 256), BF16),
            pltpu.VMEM((2, PEERS, 16, 256), BF16),
            pltpu.VMEM((8, ROWS, 128), F32),
            pltpu.VMEM((2, ROWS, D), BF16),
            pltpu.VMEM((ROWS, D), BF16),
            pltpu.VMEM((2, POS, HEADS, 64, 128), BF16),
            pltpu.VMEM((POS, 2, 128, 128), BF16),
            pltpu.VMEM((POS, KV_HEADS, 128, 128), BF16),
            pltpu.VMEM((8, ROWS, 128), BF16),
            pltpu.VMEM((2, PEERS, 16, 256), BF16),
            pltpu.VMEM((2, PEERS, 16, 256), BF16),
            pltpu.VMEM((2, ROWS, D), BF16),
            dma((7,)), dma((2, 3)), dma((2, 3)), dma((2,)), dma((2,)), dma((2,)), dma((2,)), dma((2,)),
        ],
        compiler_params=pltpu.CompilerParams(
            collective_id=0, has_side_effects=True, vmem_limit_bytes=58 * 2**20
        ),
        name="block",
    )(
        tokens.reshape(frames_here * rows_here, width), norm_space.reshape(8, 128), query_space, keyval_space,
        out_space, qk_space, norm_time.reshape(8, 128), query_time, keyval_time, out_time, qk_time,
    )


def solution(mesh):
    placed = (P("frames", "band", None), P(), P(), P(), P(), P(), P(), P(), P(), P(), P())
    return jax.shard_map(
        body, mesh=mesh, in_specs=placed, out_specs=P("frames", "band", None), check_vma=False
    )
```

```python
import functools

import jax
import jax.numpy as jnp
from jax import lax
from jax.experimental import pallas as pl
from jax.experimental.pallas import tpu as pltpu
from jax.sharding import PartitionSpec as P

HEADS = 16
KV_HEADS = 4
HEAD_DIM = 64
D = 1024
ROWS = 256
HALF = 128
PEERS = 64
POS = 4
MESH = pl.DeviceIdType.MESH
F32 = jnp.float32
BF16 = jnp.bfloat16
EXP_SCALE = 0.125 * 1.4426950408889634


def lane_half(shape):
    return lax.broadcasted_iota(jnp.int32, shape, len(shape) - 1) // HEAD_DIM


def rms_pair(tile, gain, ones_block):
    squares = tile * tile
    high = squares.astype(BF16)
    low = (squares - high.astype(F32)).astype(BF16)
    mean = jnp.dot(jnp.concatenate([high, low], axis=1), ones_block, preferred_element_type=F32)
    return tile * lax.rsqrt(mean + 1e-06) * gain


def head_queries(tile, pair):
    parity = (pair // 2) % 2
    here = lane_half(tile.shape) == parity
    turned = pltpu.roll(tile, HEAD_DIM, 1)
    first, second = (tile, turned) if parity == 0 else (turned, tile)
    zero = jnp.zeros_like(tile)
    return jnp.where(here, first, zero).astype(BF16), jnp.where(here, second, zero).astype(BF16)


def join_heads(first, second, parity):
    low = lane_half(first.shape) == 0
    if parity == 0:
        turned = pltpu.roll(second, HEAD_DIM, 1)
        over, under = jnp.where(low, first, turned), jnp.where(low, pltpu.roll(first, HEAD_DIM, 1), second)
    else:
        turned = pltpu.roll(first, HEAD_DIM, 1)
        over, under = jnp.where(low, turned, second), jnp.where(low, first, pltpu.roll(second, HEAD_DIM, 1))
    return over / under


def with_ones(tile, parity):
    return jnp.where(lane_half(tile.shape) == parity, tile, jnp.ones_like(tile))


def both_sides(tile):
    low = lane_half(tile.shape) == 0
    turned = pltpu.roll(tile, HEAD_DIM, 1)
    zero = jnp.zeros_like(tile)
    return (
        (jnp.where(low, tile, zero).astype(BF16), jnp.where(low, zero, turned).astype(BF16)),
        (jnp.where(low, turned, zero).astype(BF16), jnp.where(low, zero, tile).astype(BF16)),
    )


def pack_rows(left, right):
    peers = left.shape[0] // POS
    left = left.reshape(peers // 2, 8, 128)
    right = right.reshape(peers // 2, 8, 128)
    low = lax.broadcasted_iota(jnp.int32, left.shape, 1) < 4
    even = jnp.where(low, left, pltpu.roll(right, 4, 1))
    odd = jnp.where(low, pltpu.roll(left, 4, 1), right)
    return jnp.stack([even, odd], axis=1).reshape(peers, 8, 128)


def unpack_rows(packed):
    peers = packed.shape[0]
    packed = packed.reshape(peers // 2, 2, 8, 128)
    even, odd = packed[:, 0], packed[:, 1]
    low = lax.broadcasted_iota(jnp.int32, even.shape, 1) < 4
    left = jnp.where(low, even, pltpu.roll(odd, 4, 1))
    right = jnp.where(low, pltpu.roll(even, 4, 1), odd)
    return left.reshape(peers * POS, 128), right.reshape(peers * POS, 128)


def gain_row(ref):
    return jnp.concatenate([ref[k : k + 1, :] for k in range(8)], axis=1)


def normalise(values, gain):
    return (values * lax.rsqrt(jnp.mean(values * values, axis=-1, keepdims=True) + 1e-06) * gain).astype(BF16)


def kernel(
    tok_hbm, ns_ref, wqs_hbm, wkvs_hbm, wos_hbm, qks_ref, nt_ref, wqt_hbm, wkvt_hbm, wot_hbm, qkt_ref,
    out_hbm,
    tok, wqs, wkvs, wos, wqt, wkvt, wot,
    normed, queries, kv_all, keys_t, vals, att, send_buf, recv_buf,
    shuffle, stream_t, normed_t, queries_t, keys_time, vals_time, att_t, back_buf, home_buf, out_buf,
    load_sem, kv_send, kv_recv, a2a_send, a2a_recv, back_send, back_recv, out_sem,
):
    me = lax.axis_index("frames")
    band = lax.axis_index("band")
    my_pair = lax.div(me, 2)
    my_half = lax.rem(lax.rem(me, 2) + lax.div(my_pair, 8) + lax.rem(my_pair, 8), 2)

    def peer_of(pair, half):
        return 2 * pair + lax.rem(half + lax.div(pair, 8) + lax.rem(pair, 8), 2)

    core_peer = lax.bitwise_xor(band, 1)
    chip_peer = lax.bitwise_xor(band, 2)

    loads = {}
    for k, (name, src, dst) in enumerate(
        [("tok", tok_hbm, tok), ("wkvs", wkvs_hbm, wkvs), ("wqs", wqs_hbm, wqs), ("wos", wos_hbm, wos),
         ("wqt", wqt_hbm, wqt), ("wkvt", wkvt_hbm, wkvt), ("wot", wot_hbm, wot)]
    ):
        loads[name] = pltpu.make_async_copy(src, dst, load_sem.at[k])
        loads[name].start()

    barrier = pltpu.get_barrier_semaphore()

    def greet(k, carry):
        pl.semaphore_signal(barrier, inc=1, device_id={"frames": lax.rem(me + k, PEERS)}, device_id_type=MESH)
        return carry

    lax.fori_loop(1, PEERS, greet, 0)
    for peer in (core_peer, chip_peer):
        pl.semaphore_signal(barrier, inc=1, device_id={"band": peer}, device_id_type=MESH)

    row = lax.broadcasted_iota(jnp.int32, (256, 128), 0)
    col = lax.broadcasted_iota(jnp.int32, (256, 128), 1)
    ones_block = jnp.where((row // HEAD_DIM) % 2 == col // HEAD_DIM, 1.0 / HEAD_DIM, 0.0).astype(BF16)

    sides = jnp.where(row // 128 == col // HEAD_DIM, 1.0, 0.0).astype(BF16)
    for j in range(POS):
        for kv in range(KV_HEADS):
            vals_time[j, kv, :, 128:256] = sides

    def pair_gain(ref, k):
        return jnp.concatenate([ref[k : k + 1, :], ref[k : k + 1, :]], axis=1)

    loads["tok"].wait()
    gain_space = gain_row(ns_ref)

    def norm_rows(k, carry):
        rows = pl.ds(pl.multiple_of(k * 64, 64), 64)
        normed[rows, :] = normalise(tok[rows, :].astype(F32), gain_space)
        return carry

    lax.fori_loop(0, 2 * ROWS // 64, norm_rows, 0)

    def kv_copy(frame, slot, kind, peer):
        return pltpu.make_async_remote_copy(
            src_ref=kv_all.at[frame, slot], dst_ref=kv_all.at[frame, slot],
            send_sem=kv_send.at[frame, kind], recv_sem=kv_recv.at[frame, kind],
            device_id={"band": peer}, device_id_type=MESH)

    loads["wkvs"].wait()
    key_gain = pair_gain(qks_ref, 1)
    for frame in range(2):
        rows = slice(frame * ROWS, (frame + 1) * ROWS)
        part = jnp.dot(normed[rows, :], wkvs[...], preferred_element_type=F32)
        for t in range(2):
            tile = part[:, t * 128 : (t + 1) * 128]
            kv_all[frame, band, :, t * 128 : (t + 1) * 128] = rms_pair(tile, key_gain, ones_block).astype(BF16)
        kv_all[frame, band, :, 256:512] = part[:, 256:].astype(BF16)
        if frame == 0:
            pl.semaphore_wait(barrier, PEERS - 1 + 2)
        kv_copy(frame, band, 1, chip_peer).start()
        kv_copy(frame, band, 0, core_peer).start()

    loads["wqs"].wait()
    query_gain = pair_gain(qks_ref, 0)
    for n in range(4):
        part = jnp.dot(normed[...], wqs[:, n * 256 : (n + 1) * 256], preferred_element_type=F32)
        for k in range(2):
            pair = 2 * n + k
            tile = rms_pair(part[:, k * 128 : (k + 1) * 128], query_gain, ones_block)
            first, second = head_queries(tile, pair)
            queries[2 * pair] = first
            queries[2 * pair + 1] = second

    def forward(frame):
        kv_copy(frame, chip_peer, 1, chip_peer).wait_recv()
        kv_copy(frame, chip_peer, 2, core_peer).start()

    def space_keys(frame):
        kv_copy(frame, core_peer, 0, core_peer).wait_recv()
        kv_copy(frame, lax.bitwise_xor(band, 3), 2, core_peer).wait_recv()
        for src in range(4):
            at = slice(src * ROWS, (src + 1) * ROWS)
            for t in range(2):
                keys_t[frame, t, :, at] = kv_all[frame, src, :, t * 128 : (t + 1) * 128].T
                value_tile = kv_all[frame, src, :, 256 + t * 128 : 256 + (t + 1) * 128]
                for parity in range(2):
                    vals[frame, 2 * t + parity, at, :] = with_ones(value_tile, parity)

    def space_half(frame, half):
        start = frame * ROWS + half * HALF

        def scores_of(block):
            t, parity = block // 2, block % 2
            first = 8 * t + 4 * parity
            q = queries[first : first + 4, start : start + HALF, :].reshape(4 * HALF, 128)
            return jnp.dot(q, keys_t[frame, t], preferred_element_type=F32)

        ahead = scores_of(0)
        for block in range(4):
            t, parity = block // 2, block % 2
            scores, ahead = ahead, (scores_of(block + 1) if block < 3 else None)
            largest = jnp.max(scores, axis=-1, keepdims=True)
            weights = jnp.exp2((scores - largest) * EXP_SCALE).astype(BF16)
            done = jnp.dot(weights, vals[frame, block], preferred_element_type=F32)
            for k in range(2):
                att[2 * block + k] = join_heads(
                    done[2 * k * HALF : (2 * k + 1) * HALF], done[(2 * k + 1) * HALF : (2 * k + 2) * HALF], parity
                ).astype(BF16)

    def block_columns(left_ref, w_ref, n):
        left = jnp.concatenate([left_ref[k] for k in range(8)], axis=1)
        return jnp.dot(left, w_ref[:, n * 256 : (n + 1) * 256], preferred_element_type=F32)

    def all_of(buf, dst, frame, send_sem, recv_sem, count=PEERS - 1):
        return pltpu.make_async_remote_copy(
            src_ref=buf.at[frame, pl.ds(0, count)], dst_ref=dst.at[frame, pl.ds(0, count)],
            send_sem=send_sem, recv_sem=recv_sem, device_id={"frames": me}, device_id_type=MESH)

    def out_space(frame, half):
        start = frame * ROWS + half * HALF
        for n in range(2):
            packs = []
            for m in (n, n + 2):
                at = slice(m * 256, (m + 1) * 256)
                stream = tok[start : start + HALF, at].astype(F32) + block_columns(att, wos, m)
                stream = stream.astype(BF16).astype(F32)
                packs.append(pack_rows(stream[:, :128], stream[:, 128:]))
            send_buf[frame, half * 32 : half * 32 + 32, :, n * 128 : (n + 1) * 128] = jnp.concatenate(
                packs, axis=1).astype(BF16)

        def send(k, carry):
            pair = lax.rem(my_pair + k, 32)
            peer = peer_of(pair, half)

            @pl.when(peer != me)
            def _():
                pltpu.make_async_remote_copy(
                    src_ref=send_buf.at[frame, half * 32 + pair], dst_ref=recv_buf.at[frame, me],
                    send_sem=a2a_send.at[frame], recv_sem=a2a_recv.at[frame],
                    device_id={"frames": peer}, device_id_type=MESH).start()

            return carry

        lax.fori_loop(0, 32, send, 0)

        @pl.when(my_half == half)
        def _():
            recv_buf[frame, me] = send_buf[frame, half * 32 + my_pair]

    forward(0)
    space_keys(0)
    space_half(0, 0)
    forward(1)
    loads["wos"].wait()
    out_space(0, 0)
    space_keys(1)
    for frame, half in ((1, 0), (0, 1), (1, 1)):
        space_half(frame, half)
        out_space(frame, half)

    gain_time = gain_row(nt_ref)
    query_gain_t = pair_gain(qkt_ref, 0)
    key_gain_t = pair_gain(qkt_ref, 1)
    for name in ("wqt", "wkvt", "wot"):
        loads[name].wait()

    def arrive(frame):
        all_of(send_buf, recv_buf, frame, a2a_send.at[frame], a2a_recv.at[frame]).wait_recv()
        for n in range(2):
            pack = recv_buf[frame, :, :, n * 128 : (n + 1) * 128].astype(F32)
            for half, m in enumerate((n, n + 2)):
                left, right = unpack_rows(pack[:, half * 8 : (half + 1) * 8, :])
                shuffle[2 * m] = left
                shuffle[2 * m + 1] = right
        for j in range(POS):
            rows = slice(j * 64, (j + 1) * 64)
            values = jnp.concatenate([shuffle[k, pl.ds(j, 64, stride=4), :] for k in range(8)], axis=1)
            stream_t[frame, rows, :] = values.astype(BF16)
            normed_t[rows, :] = normalise(values, gain_time)
        hidden = normed_t[...]
        part = jnp.dot(hidden, wkvt[...], preferred_element_type=F32)
        for t in range(2):
            key_tile = rms_pair(part[:, t * 128 : (t + 1) * 128], key_gain_t, ones_block)
            value_tile = part[:, 256 + t * 128 : 256 + (t + 1) * 128]
            for kv, key_side, value_side in zip((2 * t, 2 * t + 1), both_sides(key_tile), both_sides(value_tile)):
                for side in range(2):
                    for j in range(POS):
                        rows = slice(j * 64, (j + 1) * 64)
                        keep = slice(side * 128 + frame * 64, side * 128 + frame * 64 + 64)
                        keys_time[j, kv, keep, :] = key_side[side][rows]
                        vals_time[j, kv, keep, 0:128] = value_side[side][rows]
        for n in range(4):
            part = jnp.dot(hidden, wqt[:, n * 256 : (n + 1) * 256], preferred_element_type=F32)
            for k in range(2):
                pair = 2 * n + k
                tile = rms_pair(part[:, k * 128 : (k + 1) * 128], query_gain_t, ones_block).astype(BF16)
                for j in range(POS):
                    queries_t[frame, j, pair] = tile[j * 64 : (j + 1) * 64]

    def time_half(frame):
        q_frame = 2 * (lax.broadcasted_iota(jnp.int32, (128, 128), 0) % 64) + frame
        k_row = lax.broadcasted_iota(jnp.int32, (128, 128), 1)
        allowed = q_frame >= 2 * (k_row % 64) + k_row // 64

        for j in range(POS):
            rows = slice(j * 64, (j + 1) * 64)
            for kv in range(KV_HEADS):
                q = queries_t[frame, j, 2 * kv : 2 * kv + 2].reshape(128, 128)
                scores = lax.dot_general(q, keys_time[j, kv], (((1,), (1,)), ((), ())), preferred_element_type=F32)
                weights = []
                for side in range(2):
                    mine = jnp.where(allowed, scores[:, side * 128 : (side + 1) * 128], -1e30)
                    largest = jnp.max(mine, axis=-1, keepdims=True)
                    weights.append(jnp.exp2((mine - largest) * EXP_SCALE).astype(BF16))
                done = jnp.dot(jnp.concatenate(weights, axis=1), vals_time[j, kv], preferred_element_type=F32)
                out = (done[:, :128] / done[:, 128:]).astype(BF16)
                att_t[2 * kv, rows, :] = out[:64]
                att_t[2 * kv + 1, rows, :] = out[64:]
        for n in range(4):
            at = slice(n * 256, (n + 1) * 256)
            mixed = stream_t[frame, :, at].astype(F32) + block_columns(att_t, wot, n)
            mixed = mixed.astype(BF16).astype(F32)
            for j in range(POS):
                for half in range(2):
                    shuffle[2 * n + half, pl.ds(j, 64, stride=4), :] = mixed[
                        j * 64 : (j + 1) * 64, half * 128 : (half + 1) * 128]
        for n in range(2):
            packs = [pack_rows(shuffle[2 * m], shuffle[2 * m + 1]) for m in (n, n + 2)]
            back_buf[frame, :, :, n * 128 : (n + 1) * 128] = jnp.concatenate(packs, axis=1).astype(BF16)

        def send(k, carry):
            peer = lax.rem(me + k, PEERS)
            pltpu.make_async_remote_copy(
                src_ref=back_buf.at[frame, peer], dst_ref=home_buf.at[frame, my_half * 32 + my_pair],
                send_sem=back_send.at[frame], recv_sem=back_recv.at[frame, my_half],
                device_id={"frames": peer}, device_id_type=MESH).start()
            return carry

        lax.fori_loop(1, PEERS, send, 0)
        home_buf[frame, my_half * 32 + my_pair] = back_buf[frame, me]

    arrive(0)
    arrive(1)
    time_half(0)
    time_half(1)

    def finish(frame, half):
        for count in (31, 32):
            @pl.when(my_half == half if count == 31 else my_half != half)
            def _():
                all_of(back_buf, home_buf, frame, back_send.at[frame], back_recv.at[frame, half], count).wait_recv()

        rows = slice(half * HALF, (half + 1) * HALF)
        for n in range(2):
            pack = home_buf[frame, half * 32 : half * 32 + 32, :, n * 128 : (n + 1) * 128].astype(F32)
            for part, m in enumerate((n, n + 2)):
                left, right = unpack_rows(pack[:, part * 8 : (part + 1) * 8, :])
                out_buf[frame, rows, m * 256 : m * 256 + 128] = left.astype(BF16)
                out_buf[frame, rows, m * 256 + 128 : (m + 1) * 256] = right.astype(BF16)
        copy = pltpu.make_async_copy(out_buf.at[frame, rows], out_hbm.at[frame, rows], out_sem.at[frame, half])
        copy.start()
        return copy

    copies = [finish(0, 0), finish(1, 0), finish(0, 1), finish(1, 1)]
    for frame in range(2):
        kv_copy(frame, band, 0, core_peer).wait_send()
        kv_copy(frame, band, 1, chip_peer).wait_send()
        kv_copy(frame, chip_peer, 2, core_peer).wait_send()
        all_of(send_buf, recv_buf, frame, a2a_send.at[frame], a2a_recv.at[frame]).wait_send()
        all_of(back_buf, home_buf, frame, back_send.at[frame], back_recv.at[frame, 0]).wait_send()
    for copy in copies:
        copy.wait()


def body(tokens, norm_space, query_space, keyval_space, out_space, qk_space,
         norm_time, query_time, keyval_time, out_time, qk_time):
    frames_here, rows_here, width = tokens.shape
    any_spec = pl.BlockSpec(memory_space=pl.ANY)
    vmem = pl.BlockSpec(memory_space=pltpu.VMEM)
    dma = pltpu.SemaphoreType.DMA
    return pl.pallas_call(
        kernel,
        out_shape=jax.ShapeDtypeStruct((frames_here, rows_here, width), BF16),
        in_specs=[any_spec, vmem, any_spec, any_spec, any_spec, vmem, vmem, any_spec, any_spec, any_spec, vmem],
        out_specs=any_spec,
        scratch_shapes=[
            pltpu.VMEM((2 * ROWS, D), BF16),
            pltpu.VMEM((D, D), BF16), pltpu.VMEM((D, 512), BF16), pltpu.VMEM((D, D), BF16),
            pltpu.VMEM((D, D), BF16), pltpu.VMEM((D, 512), BF16), pltpu.VMEM((D, D), BF16),
            pltpu.VMEM((2 * ROWS, D), BF16),
            pltpu.VMEM((HEADS, 2 * ROWS, 128), BF16),
            pltpu.VMEM((2, 4, ROWS, 512), BF16),
            pltpu.VMEM((2, 2, 128, 4 * ROWS), BF16),
            pltpu.VMEM((2, KV_HEADS, 4 * ROWS, 128), BF16),
            pltpu.VMEM((8, HALF, 128), BF16),
            pltpu.VMEM((2, PEERS, 16, 256), BF16),
            pltpu.VMEM((2, PEERS, 16, 256), BF16),
            pltpu.VMEM((8, ROWS, 128), F32),
            pltpu.VMEM((2, ROWS, D), BF16),
            pltpu.VMEM((ROWS, D), BF16),
            pltpu.VMEM((2, POS, HEADS // 2, 64, 128), BF16),
            pltpu.VMEM((POS, KV_HEADS, 256, 128), BF16),
            pltpu.VMEM((POS, KV_HEADS, 256, 256), BF16),
            pltpu.VMEM((8, ROWS, 128), BF16),
            pltpu.VMEM((2, PEERS, 16, 256), BF16),
            pltpu.VMEM((2, PEERS, 16, 256), BF16),
            pltpu.VMEM((2, ROWS, D), BF16),
            dma((7,)), dma((2, 3)), dma((2, 3)), dma((2,)), dma((2,)), dma((2,)), dma((2, 2)), dma((2, 2)),
        ],
        compiler_params=pltpu.CompilerParams(
            collective_id=0, has_side_effects=True, vmem_limit_bytes=58 * 2**20
        ),
        name="block",
    )(
        tokens.reshape(frames_here * rows_here, width), norm_space.reshape(8, 128), query_space, keyval_space,
        out_space, qk_space, norm_time.reshape(8, 128), query_time, keyval_time, out_time, qk_time,
    )


def solution(mesh):
    placed = (P("frames", "band", None), P(), P(), P(), P(), P(), P(), P(), P(), P(), P())
    return jax.shard_map(
        body, mesh=mesh, in_specs=placed, out_specs=P("frames", "band", None), check_vma=False
    )
```

```python
import functools

import jax
import jax.numpy as jnp
from jax import lax
from jax.experimental import pallas as pl
from jax.experimental.pallas import tpu as pltpu
from jax.sharding import PartitionSpec as P

HEADS = 16
KV_HEADS = 4
HEAD_DIM = 64
D = 1024
ROWS = 256
HALF = 128
PEERS = 64
POS = 4
MESH = pl.DeviceIdType.MESH
F32 = jnp.float32
BF16 = jnp.bfloat16
EXP_SCALE = 0.125 * 1.4426950408889634


def lane_half(shape):
    return lax.broadcasted_iota(jnp.int32, shape, len(shape) - 1) // HEAD_DIM


def rms_pair(tile, gain, ones_block):
    squares = tile * tile
    high = squares.astype(BF16)
    low = (squares - high.astype(F32)).astype(BF16)
    mean = jnp.dot(jnp.concatenate([high, low], axis=1), ones_block, preferred_element_type=F32)
    return tile * lax.rsqrt(mean + 1e-06) * gain


def head_queries(tile, pair):
    parity = (pair // 2) % 2
    here = lane_half(tile.shape) == parity
    turned = pltpu.roll(tile, HEAD_DIM, 1)
    first, second = (tile, turned) if parity == 0 else (turned, tile)
    zero = jnp.zeros_like(tile)
    return jnp.where(here, first, zero).astype(BF16), jnp.where(here, second, zero).astype(BF16)


def join_heads(first, second, parity):
    low = lane_half(first.shape) == 0
    if parity == 0:
        turned = pltpu.roll(second, HEAD_DIM, 1)
        over, under = jnp.where(low, first, turned), jnp.where(low, pltpu.roll(first, HEAD_DIM, 1), second)
    else:
        turned = pltpu.roll(first, HEAD_DIM, 1)
        over, under = jnp.where(low, turned, second), jnp.where(low, first, pltpu.roll(second, HEAD_DIM, 1))
    return over / under


def with_ones(tile, parity):
    return jnp.where(lane_half(tile.shape) == parity, tile, jnp.ones_like(tile))


def both_sides(tile):
    low = lane_half(tile.shape) == 0
    turned = pltpu.roll(tile, HEAD_DIM, 1)
    zero = jnp.zeros_like(tile)
    return (
        (jnp.where(low, tile, zero).astype(BF16), jnp.where(low, zero, turned).astype(BF16)),
        (jnp.where(low, turned, zero).astype(BF16), jnp.where(low, zero, tile).astype(BF16)),
    )


def pack_rows(left, right):
    peers = left.shape[0] // POS
    left = left.reshape(peers // 2, 8, 128)
    right = right.reshape(peers // 2, 8, 128)
    low = lax.broadcasted_iota(jnp.int32, left.shape, 1) < 4
    even = jnp.where(low, left, pltpu.roll(right, 4, 1))
    odd = jnp.where(low, pltpu.roll(left, 4, 1), right)
    return jnp.stack([even, odd], axis=1).reshape(peers, 8, 128)


def unpack_rows(packed):
    peers = packed.shape[0]
    packed = packed.reshape(peers // 2, 2, 8, 128)
    even, odd = packed[:, 0], packed[:, 1]
    low = lax.broadcasted_iota(jnp.int32, even.shape, 1) < 4
    left = jnp.where(low, even, pltpu.roll(odd, 4, 1))
    right = jnp.where(low, pltpu.roll(even, 4, 1), odd)
    return left.reshape(peers * POS, 128), right.reshape(peers * POS, 128)


def gain_row(ref):
    return jnp.concatenate([ref[k : k + 1, :] for k in range(8)], axis=1)


def normalise(values, gain):
    return (values * lax.rsqrt(jnp.mean(values * values, axis=-1, keepdims=True) + 1e-06) * gain).astype(BF16)


def kernel(
    tok_hbm, ns_ref, wqs_hbm, wkvs_hbm, wos_hbm, qks_ref, nt_ref, wqt_hbm, wkvt_hbm, wot_hbm, qkt_ref,
    out_hbm,
    tok, wqs, wkvs, wos, wqt, wkvt, wot,
    normed, queries, kv_all, keys_t, vals, att, send_buf, recv_buf,
    shuffle, stream_t, normed_t, queries_t, keys_time, vals_time, att_t, back_buf, home_buf, out_buf,
    load_sem, kv_send, kv_recv, a2a_send, a2a_recv, back_send, back_recv, out_sem,
):
    me = lax.axis_index("frames")
    band = lax.axis_index("band")
    my_pair = lax.div(me, 2)
    my_half = lax.rem(lax.rem(me, 2) + lax.div(my_pair, 8) + lax.rem(my_pair, 8), 2)

    def peer_of(pair, half):
        return 2 * pair + lax.rem(half + lax.div(pair, 8) + lax.rem(pair, 8), 2)

    core_peer = lax.bitwise_xor(band, 1)
    chip_peer = lax.bitwise_xor(band, 2)

    loads = {}
    for k, (name, src, dst) in enumerate(
        [("tok", tok_hbm, tok), ("wkvs", wkvs_hbm, wkvs), ("wqs", wqs_hbm, wqs), ("wos", wos_hbm, wos),
         ("wqt", wqt_hbm, wqt), ("wkvt", wkvt_hbm, wkvt), ("wot", wot_hbm, wot)]
    ):
        loads[name] = pltpu.make_async_copy(src, dst, load_sem.at[k])
    loads["tok"].start()
    loads["wkvs"].start()

    barrier = pltpu.get_barrier_semaphore()

    def greet(k, carry):
        pl.semaphore_signal(barrier, inc=1, device_id={"frames": lax.rem(me + k, PEERS)}, device_id_type=MESH)
        return carry

    lax.fori_loop(1, PEERS, greet, 0)
    for peer in (core_peer, chip_peer):
        pl.semaphore_signal(barrier, inc=1, device_id={"band": peer}, device_id_type=MESH)

    row = lax.broadcasted_iota(jnp.int32, (256, 128), 0)
    col = lax.broadcasted_iota(jnp.int32, (256, 128), 1)
    ones_block = jnp.where((row // HEAD_DIM) % 2 == col // HEAD_DIM, 1.0 / HEAD_DIM, 0.0).astype(BF16)

    sides = jnp.where(row // 128 == col // HEAD_DIM, 1.0, 0.0).astype(BF16)
    for j in range(POS):
        for kv in range(KV_HEADS):
            vals_time[j, kv, :, 128:256] = sides

    def pair_gain(ref, k):
        return jnp.concatenate([ref[k : k + 1, :], ref[k : k + 1, :]], axis=1)

    loads["tok"].wait()
    gain_space = gain_row(ns_ref)

    for name in ("wqs", "wos", "wqt", "wkvt", "wot"):
        loads[name].start()

    def kv_copy(frame, t, slot, kind, peer):
        return pltpu.make_async_remote_copy(
            src_ref=kv_all.at[frame, t, slot], dst_ref=kv_all.at[frame, t, slot],
            send_sem=kv_send.at[frame, t, kind], recv_sem=kv_recv.at[frame, t, kind],
            device_id={"band": peer}, device_id_type=MESH)

    key_gain = pair_gain(qks_ref, 1)
    for frame in range(2):
        def norm_rows(k, carry):
            rows = pl.ds(pl.multiple_of(frame * ROWS + k * 64, 64), 64)
            normed[rows, :] = normalise(tok[rows, :].astype(F32), gain_space)
            return carry

        lax.fori_loop(0, ROWS // 64, norm_rows, 0)
        if frame == 0:
            loads["wkvs"].wait()
        rows = slice(frame * ROWS, (frame + 1) * ROWS)
        part = jnp.dot(normed[rows, :], wkvs[...], preferred_element_type=F32)
        for t in range(2):
            tile = part[:, t * 128 : (t + 1) * 128]
            kv_all[frame, t, band, :, 0:128] = rms_pair(tile, key_gain, ones_block).astype(BF16)
            kv_all[frame, t, band, :, 128:256] = part[:, 256 + t * 128 : 256 + (t + 1) * 128].astype(BF16)
        if frame == 0:
            pl.semaphore_wait(barrier, PEERS - 1 + 2)
        for t in range(2):
            kv_copy(frame, t, band, 1, chip_peer).start()
            kv_copy(frame, t, band, 0, core_peer).start()

    loads["wqs"].wait()
    query_gain = pair_gain(qks_ref, 0)
    for n in range(4):
        part = jnp.dot(normed[...], wqs[:, n * 256 : (n + 1) * 256], preferred_element_type=F32)
        for k in range(2):
            pair = 2 * n + k
            tile = rms_pair(part[:, k * 128 : (k + 1) * 128], query_gain, ones_block)
            first, second = head_queries(tile, pair)
            queries[2 * pair] = first
            queries[2 * pair + 1] = second

    def forward(frame, t):
        kv_copy(frame, t, chip_peer, 1, chip_peer).wait_recv()
        kv_copy(frame, t, chip_peer, 2, core_peer).start()

    def space_keys(frame, t):
        kv_copy(frame, t, core_peer, 0, core_peer).wait_recv()
        for k in range(4):
            src = lax.bitwise_xor(band, k)
            if k == 3:
                kv_copy(frame, t, src, 2, core_peer).wait_recv()
            at = slice(k * ROWS, (k + 1) * ROWS)
            keys_t[frame, t, :, at] = kv_all[frame, t, src, :, 0:128].T
            value_tile = kv_all[frame, t, src, :, 128:256]
            for parity in range(2):
                vals[frame, 2 * t + parity, at, :] = with_ones(value_tile, parity)

    def space_half(frame, half, blocks):
        start = frame * ROWS + half * HALF

        def scores_of(block):
            q = queries[4 * block : 4 * block + 4, start : start + HALF, :].reshape(4 * HALF, 128)
            return jnp.dot(q, keys_t[frame, block // 2], preferred_element_type=F32)

        ahead = scores_of(blocks[0])
        for block in blocks:
            parity = block % 2
            scores, ahead = ahead, (scores_of(block + 1) if block != blocks[-1] else None)
            largest = jnp.max(scores, axis=-1, keepdims=True)
            weights = jnp.exp2((scores - largest) * EXP_SCALE).astype(BF16)
            done = jnp.dot(weights, vals[frame, block], preferred_element_type=F32)
            for k in range(2):
                att[half, 2 * block + k] = join_heads(
                    done[2 * k * HALF : (2 * k + 1) * HALF], done[(2 * k + 1) * HALF : (2 * k + 2) * HALF], parity
                ).astype(BF16)

    def block_columns(left_ref, w_ref, n):
        left = jnp.concatenate([left_ref[k] for k in range(8)], axis=1)
        return jnp.dot(left, w_ref[:, n * 256 : (n + 1) * 256], preferred_element_type=F32)

    def all_of(buf, dst, frame, send_sem, recv_sem, count=PEERS - 1):
        return pltpu.make_async_remote_copy(
            src_ref=buf.at[frame, pl.ds(0, count)], dst_ref=dst.at[frame, pl.ds(0, count)],
            send_sem=send_sem, recv_sem=recv_sem, device_id={"frames": me}, device_id_type=MESH)

    def out_space(frame, half):
        start = frame * ROWS + half * HALF
        for n in range(2):
            packs = []
            for m in (n, n + 2):
                at = slice(m * 256, (m + 1) * 256)
                stream = tok[start : start + HALF, at].astype(F32) + block_columns(att.at[half], wos, m)
                stream = stream.astype(BF16).astype(F32)
                packs.append(pack_rows(stream[:, :128], stream[:, 128:]))
            send_buf[frame, half * 32 : half * 32 + 32, :, n * 128 : (n + 1) * 128] = jnp.concatenate(
                packs, axis=1).astype(BF16)

        def send(k, carry):
            pair = lax.rem(my_pair + k, 32)
            peer = peer_of(pair, half)

            @pl.when(peer != me)
            def _():
                pltpu.make_async_remote_copy(
                    src_ref=send_buf.at[frame, half * 32 + pair], dst_ref=recv_buf.at[frame, me],
                    send_sem=a2a_send.at[frame], recv_sem=a2a_recv.at[frame],
                    device_id={"frames": peer}, device_id_type=MESH).start()

            return carry

        lax.fori_loop(0, 32, send, 0)

        @pl.when(my_half == half)
        def _():
            recv_buf[frame, me] = send_buf[frame, half * 32 + my_pair]

    forward(0, 0)
    space_keys(0, 0)
    space_half(0, 0, (0, 1))
    forward(0, 1)
    space_half(0, 1, (0, 1))
    space_keys(0, 1)
    space_half(0, 0, (2, 3))
    loads["wos"].wait()
    out_space(0, 0)
    forward(1, 0)
    space_half(0, 1, (2, 3))
    out_space(0, 1)
    forward(1, 1)
    space_keys(1, 0)
    space_keys(1, 1)
    for half in range(2):
        space_half(1, half, (0, 1, 2, 3))
        out_space(1, half)

    gain_time = gain_row(nt_ref)
    query_gain_t = pair_gain(qkt_ref, 0)
    key_gain_t = pair_gain(qkt_ref, 1)
    for name in ("wqt", "wkvt", "wot"):
        loads[name].wait()

    def arrive(frame):
        all_of(send_buf, recv_buf, frame, a2a_send.at[frame], a2a_recv.at[frame]).wait_recv()
        for n in range(2):
            pack = recv_buf[frame, :, :, n * 128 : (n + 1) * 128].astype(F32)
            for half, m in enumerate((n, n + 2)):
                left, right = unpack_rows(pack[:, half * 8 : (half + 1) * 8, :])
                shuffle[2 * m] = left
                shuffle[2 * m + 1] = right
        for j in range(POS):
            rows = slice(j * 64, (j + 1) * 64)
            values = jnp.concatenate([shuffle[k, pl.ds(j, 64, stride=4), :] for k in range(8)], axis=1)
            stream_t[frame, rows, :] = values.astype(BF16)
            normed_t[rows, :] = normalise(values, gain_time)
        hidden = normed_t[...]
        part = jnp.dot(hidden, wkvt[...], preferred_element_type=F32)
        for t in range(2):
            key_tile = rms_pair(part[:, t * 128 : (t + 1) * 128], key_gain_t, ones_block)
            value_tile = part[:, 256 + t * 128 : 256 + (t + 1) * 128]
            for kv, key_side, value_side in zip((2 * t, 2 * t + 1), both_sides(key_tile), both_sides(value_tile)):
                for side in range(2):
                    for j in range(POS):
                        rows = slice(j * 64, (j + 1) * 64)
                        keep = slice(side * 128 + frame * 64, side * 128 + frame * 64 + 64)
                        keys_time[j, kv, keep, :] = key_side[side][rows]
                        vals_time[j, kv, keep, 0:128] = value_side[side][rows]
        for n in range(4):
            part = jnp.dot(hidden, wqt[:, n * 256 : (n + 1) * 256], preferred_element_type=F32)
            for k in range(2):
                pair = 2 * n + k
                tile = rms_pair(part[:, k * 128 : (k + 1) * 128], query_gain_t, ones_block).astype(BF16)
                for j in range(POS):
                    queries_t[frame, j, pair] = tile[j * 64 : (j + 1) * 64]

    def time_half(frame):
        q_frame = 2 * (lax.broadcasted_iota(jnp.int32, (128, 128), 0) % 64) + frame
        k_row = lax.broadcasted_iota(jnp.int32, (128, 128), 1)
        allowed = q_frame >= 2 * (k_row % 64) + k_row // 64

        for j in range(POS):
            rows = slice(j * 64, (j + 1) * 64)
            for kv in range(KV_HEADS):
                q = queries_t[frame, j, 2 * kv : 2 * kv + 2].reshape(128, 128)
                scores = lax.dot_general(q, keys_time[j, kv], (((1,), (1,)), ((), ())), preferred_element_type=F32)
                weights = []
                for side in range(2):
                    mine = jnp.where(allowed, scores[:, side * 128 : (side + 1) * 128], -1e30)
                    largest = jnp.max(mine, axis=-1, keepdims=True)
                    weights.append(jnp.exp2((mine - largest) * EXP_SCALE).astype(BF16))
                done = jnp.dot(jnp.concatenate(weights, axis=1), vals_time[j, kv], preferred_element_type=F32)
                out = (done[:, :128] / done[:, 128:]).astype(BF16)
                att_t[2 * kv, rows, :] = out[:64]
                att_t[2 * kv + 1, rows, :] = out[64:]
        for n in range(4):
            at = slice(n * 256, (n + 1) * 256)
            mixed = stream_t[frame, :, at].astype(F32) + block_columns(att_t, wot, n)
            mixed = mixed.astype(BF16).astype(F32)
            for j in range(POS):
                for half in range(2):
                    shuffle[2 * n + half, pl.ds(j, 64, stride=4), :] = mixed[
                        j * 64 : (j + 1) * 64, half * 128 : (half + 1) * 128]
        for n in range(2):
            packs = [pack_rows(shuffle[2 * m], shuffle[2 * m + 1]) for m in (n, n + 2)]
            back_buf[frame, :, :, n * 128 : (n + 1) * 128] = jnp.concatenate(packs, axis=1).astype(BF16)

        def send(k, carry):
            peer = lax.rem(me + k, PEERS)
            pltpu.make_async_remote_copy(
                src_ref=back_buf.at[frame, peer], dst_ref=home_buf.at[frame, my_half * 32 + my_pair],
                send_sem=back_send.at[frame], recv_sem=back_recv.at[frame, my_half],
                device_id={"frames": peer}, device_id_type=MESH).start()
            return carry

        lax.fori_loop(1, PEERS, send, 0)
        home_buf[frame, my_half * 32 + my_pair] = back_buf[frame, me]

    arrive(0)
    arrive(1)
    time_half(0)
    time_half(1)

    def finish(frame, half):
        for count in (31, 32):
            @pl.when(my_half == half if count == 31 else my_half != half)
            def _():
                all_of(back_buf, home_buf, frame, back_send.at[frame], back_recv.at[frame, half], count).wait_recv()

        rows = slice(half * HALF, (half + 1) * HALF)
        for n in range(2):
            pack = home_buf[frame, half * 32 : half * 32 + 32, :, n * 128 : (n + 1) * 128].astype(F32)
            for part, m in enumerate((n, n + 2)):
                left, right = unpack_rows(pack[:, part * 8 : (part + 1) * 8, :])
                out_buf[frame, rows, m * 256 : m * 256 + 128] = left.astype(BF16)
                out_buf[frame, rows, m * 256 + 128 : (m + 1) * 256] = right.astype(BF16)
        copy = pltpu.make_async_copy(out_buf.at[frame, rows], out_hbm.at[frame, rows], out_sem.at[frame, half])
        copy.start()
        return copy

    copies = [finish(0, 0), finish(1, 0), finish(0, 1), finish(1, 1)]
    for frame in range(2):
        for t in range(2):
            kv_copy(frame, t, band, 0, core_peer).wait_send()
            kv_copy(frame, t, band, 1, chip_peer).wait_send()
            kv_copy(frame, t, chip_peer, 2, core_peer).wait_send()
        all_of(send_buf, recv_buf, frame, a2a_send.at[frame], a2a_recv.at[frame]).wait_send()
        all_of(back_buf, home_buf, frame, back_send.at[frame], back_recv.at[frame, 0]).wait_send()
    for copy in copies:
        copy.wait()


def body(tokens, norm_space, query_space, keyval_space, out_space, qk_space,
         norm_time, query_time, keyval_time, out_time, qk_time):
    frames_here, rows_here, width = tokens.shape
    any_spec = pl.BlockSpec(memory_space=pl.ANY)
    vmem = pl.BlockSpec(memory_space=pltpu.VMEM)
    dma = pltpu.SemaphoreType.DMA
    return pl.pallas_call(
        kernel,
        out_shape=jax.ShapeDtypeStruct((frames_here, rows_here, width), BF16),
        in_specs=[any_spec, vmem, any_spec, any_spec, any_spec, vmem, vmem, any_spec, any_spec, any_spec, vmem],
        out_specs=any_spec,
        scratch_shapes=[
            pltpu.VMEM((2 * ROWS, D), BF16),
            pltpu.VMEM((D, D), BF16), pltpu.VMEM((D, 512), BF16), pltpu.VMEM((D, D), BF16),
            pltpu.VMEM((D, D), BF16), pltpu.VMEM((D, 512), BF16), pltpu.VMEM((D, D), BF16),
            pltpu.VMEM((2 * ROWS, D), BF16),
            pltpu.VMEM((HEADS, 2 * ROWS, 128), BF16),
            pltpu.VMEM((2, 2, 4, ROWS, 256), BF16),
            pltpu.VMEM((2, 2, 128, 4 * ROWS), BF16),
            pltpu.VMEM((2, KV_HEADS, 4 * ROWS, 128), BF16),
            pltpu.VMEM((2, 8, HALF, 128), BF16),
            pltpu.VMEM((2, PEERS, 16, 256), BF16),
            pltpu.VMEM((2, PEERS, 16, 256), BF16),
            pltpu.VMEM((8, ROWS, 128), F32),
            pltpu.VMEM((2, ROWS, D), BF16),
            pltpu.VMEM((ROWS, D), BF16),
            pltpu.VMEM((2, POS, HEADS // 2, 64, 128), BF16),
            pltpu.VMEM((POS, KV_HEADS, 256, 128), BF16),
            pltpu.VMEM((POS, KV_HEADS, 256, 256), BF16),
            pltpu.VMEM((8, ROWS, 128), BF16),
            pltpu.VMEM((2, PEERS, 16, 256), BF16),
            pltpu.VMEM((2, PEERS, 16, 256), BF16),
            pltpu.VMEM((2, ROWS, D), BF16),
            dma((7,)), dma((2, 2, 3)), dma((2, 2, 3)), dma((2,)), dma((2,)), dma((2,)), dma((2, 2)), dma((2, 2)),
        ],
        compiler_params=pltpu.CompilerParams(
            collective_id=0, has_side_effects=True, vmem_limit_bytes=58 * 2**20
        ),
        name="block",
    )(
        tokens.reshape(frames_here * rows_here, width), norm_space.reshape(8, 128), query_space, keyval_space,
        out_space, qk_space, norm_time.reshape(8, 128), query_time, keyval_time, out_time, qk_time,
    )


def solution(mesh):
    placed = (P("frames", "band", None), P(), P(), P(), P(), P(), P(), P(), P(), P(), P())
    return jax.shard_map(
        body, mesh=mesh, in_specs=placed, out_specs=P("frames", "band", None), check_vma=False
    )
```

```python
import functools

import jax
import jax.numpy as jnp
from jax import lax
from jax.experimental import pallas as pl
from jax.experimental.pallas import tpu as pltpu
from jax.sharding import PartitionSpec as P

HEADS = 16
KV_HEADS = 4
HEAD_DIM = 64
D = 1024
ROWS = 256
HALF = 128
PEERS = 64
POS = 4
MESH = pl.DeviceIdType.MESH
F32 = jnp.float32
BF16 = jnp.bfloat16
EXP_SCALE = 0.125 * 1.4426950408889634


def lane_half(shape):
    return lax.broadcasted_iota(jnp.int32, shape, len(shape) - 1) // HEAD_DIM


def rms_pair(tile, gain, ones_block):
    squares = tile * tile
    high = squares.astype(BF16)
    low = (squares - high.astype(F32)).astype(BF16)
    mean = jnp.dot(jnp.concatenate([high, low], axis=1), ones_block, preferred_element_type=F32)
    return tile * lax.rsqrt(mean + 1e-06) * gain


def head_queries(tile, pair):
    parity = (pair // 2) % 2
    here = lane_half(tile.shape) == parity
    turned = pltpu.roll(tile, HEAD_DIM, 1)
    first, second = (tile, turned) if parity == 0 else (turned, tile)
    zero = jnp.zeros_like(tile)
    return jnp.where(here, first, zero).astype(BF16), jnp.where(here, second, zero).astype(BF16)


def join_heads(first, second, parity):
    low = lane_half(first.shape) == 0
    if parity == 0:
        turned = pltpu.roll(second, HEAD_DIM, 1)
        over, under = jnp.where(low, first, turned), jnp.where(low, pltpu.roll(first, HEAD_DIM, 1), second)
    else:
        turned = pltpu.roll(first, HEAD_DIM, 1)
        over, under = jnp.where(low, turned, second), jnp.where(low, first, pltpu.roll(second, HEAD_DIM, 1))
    return over / under


def with_ones(tile, parity):
    return jnp.where(lane_half(tile.shape) == parity, tile, jnp.ones_like(tile))


def both_sides(tile):
    low = lane_half(tile.shape) == 0
    turned = pltpu.roll(tile, HEAD_DIM, 1)
    zero = jnp.zeros_like(tile)
    return (
        (jnp.where(low, tile, zero).astype(BF16), jnp.where(low, zero, turned).astype(BF16)),
        (jnp.where(low, turned, zero).astype(BF16), jnp.where(low, zero, tile).astype(BF16)),
    )


def pack_rows(left, right):
    peers = left.shape[0] // POS
    left = left.reshape(peers // 2, 8, 128)
    right = right.reshape(peers // 2, 8, 128)
    low = lax.broadcasted_iota(jnp.int32, left.shape, 1) < 4
    even = jnp.where(low, left, pltpu.roll(right, 4, 1))
    odd = jnp.where(low, pltpu.roll(left, 4, 1), right)
    return jnp.stack([even, odd], axis=1).reshape(peers, 8, 128)


def unpack_rows(packed):
    peers = packed.shape[0]
    packed = packed.reshape(peers // 2, 2, 8, 128)
    even, odd = packed[:, 0], packed[:, 1]
    low = lax.broadcasted_iota(jnp.int32, even.shape, 1) < 4
    left = jnp.where(low, even, pltpu.roll(odd, 4, 1))
    right = jnp.where(low, pltpu.roll(even, 4, 1), odd)
    return left.reshape(peers * POS, 128), right.reshape(peers * POS, 128)


def gain_row(ref):
    return jnp.concatenate([ref[k : k + 1, :] for k in range(8)], axis=1)


def normalise(values, gain):
    return (values * lax.rsqrt(jnp.mean(values * values, axis=-1, keepdims=True) + 1e-06) * gain).astype(BF16)


def kernel(
    tok_hbm, ns_ref, wqs_hbm, wkvs_hbm, wos_hbm, qks_ref, nt_ref, wqt_hbm, wkvt_hbm, wot_hbm, qkt_ref,
    out_hbm,
    tok, wqs, wkvs, wos, wqt, wkvt, wot,
    normed, queries, kv_all, keys_t, vals, att, send_buf, recv_buf,
    shuffle, stream_t, normed_t, queries_t, keys_time, vals_time, att_t, back_buf, home_buf, out_buf,
    load_sem, kv_send, kv_recv, a2a_send, a2a_recv, back_send, back_recv, out_sem,
):
    me = lax.axis_index("frames")
    band = lax.axis_index("band")
    my_pair = lax.div(me, 2)
    my_half = lax.rem(lax.rem(me, 2) + lax.div(my_pair, 8) + lax.rem(my_pair, 8), 2)

    def peer_of(pair, half):
        return 2 * pair + lax.rem(half + lax.div(pair, 8) + lax.rem(pair, 8), 2)

    core_peer = lax.bitwise_xor(band, 1)
    chip_peer = lax.bitwise_xor(band, 2)

    loads = {}
    for k, (name, src, dst) in enumerate(
        [("tok", tok_hbm, tok), ("wkvs", wkvs_hbm, wkvs), ("wqs", wqs_hbm, wqs), ("wos", wos_hbm, wos),
         ("wqt", wqt_hbm, wqt), ("wkvt", wkvt_hbm, wkvt), ("wot", wot_hbm, wot)]
    ):
        loads[name] = pltpu.make_async_copy(src, dst, load_sem.at[k])
    loads["tok"].start()
    loads["wkvs"].start()

    barrier = pltpu.get_barrier_semaphore()

    def greet(k, carry):
        pl.semaphore_signal(barrier, inc=1, device_id={"frames": lax.rem(me + k, PEERS)}, device_id_type=MESH)
        return carry

    lax.fori_loop(1, PEERS, greet, 0)
    for peer in (core_peer, chip_peer):
        pl.semaphore_signal(barrier, inc=1, device_id={"band": peer}, device_id_type=MESH)

    row = lax.broadcasted_iota(jnp.int32, (256, 128), 0)
    col = lax.broadcasted_iota(jnp.int32, (256, 128), 1)
    ones_block = jnp.where((row // HEAD_DIM) % 2 == col // HEAD_DIM, 1.0 / HEAD_DIM, 0.0).astype(BF16)

    sides = jnp.where(row // 128 == col // HEAD_DIM, 1.0, 0.0).astype(BF16)
    for j in range(POS):
        for kv in range(KV_HEADS):
            vals_time[j, kv, :, 128:256] = sides

    def pair_gain(ref, k):
        return jnp.concatenate([ref[k : k + 1, :], ref[k : k + 1, :]], axis=1)

    loads["tok"].wait()
    gain_space = gain_row(ns_ref)

    for name in ("wqs", "wos", "wqt", "wkvt", "wot"):
        loads[name].start()

    def kv_copy(frame, t, slot, kind, peer):
        return pltpu.make_async_remote_copy(
            src_ref=kv_all.at[frame, t, slot], dst_ref=kv_all.at[frame, t, slot],
            send_sem=kv_send.at[frame, t, kind], recv_sem=kv_recv.at[frame, t, kind],
            device_id={"band": peer}, device_id_type=MESH)

    key_gain = pair_gain(qks_ref, 1)
    for frame in range(2):
        def norm_rows(k, carry):
            rows = pl.ds(pl.multiple_of(frame * ROWS + k * 64, 64), 64)
            normed[rows, :] = normalise(tok[rows, :].astype(F32), gain_space)
            return carry

        lax.fori_loop(0, ROWS // 64, norm_rows, 0)
        if frame == 0:
            loads["wkvs"].wait()
        rows = slice(frame * ROWS, (frame + 1) * ROWS)
        part = jnp.dot(normed[rows, :], wkvs[...], preferred_element_type=F32)
        for t in range(2):
            tile = part[:, t * 128 : (t + 1) * 128]
            kv_all[frame, t, band, :, 0:128] = rms_pair(tile, key_gain, ones_block).astype(BF16)
            kv_all[frame, t, band, :, 128:256] = part[:, 256 + t * 128 : 256 + (t + 1) * 128].astype(BF16)
        if frame == 0:
            pl.semaphore_wait(barrier, PEERS - 1 + 2)
        for t in range(2):
            kv_copy(frame, t, band, 1, chip_peer).start()
            kv_copy(frame, t, band, 0, core_peer).start()

    loads["wqs"].wait()
    query_gain = pair_gain(qks_ref, 0)
    for n in range(4):
        part = jnp.dot(normed[...], wqs[:, n * 256 : (n + 1) * 256], preferred_element_type=F32)
        for k in range(2):
            pair = 2 * n + k
            tile = rms_pair(part[:, k * 128 : (k + 1) * 128], query_gain, ones_block)
            first, second = head_queries(tile, pair)
            queries[2 * pair] = first
            queries[2 * pair + 1] = second

    def forward(frame, t):
        kv_copy(frame, t, chip_peer, 1, chip_peer).wait_recv()
        kv_copy(frame, t, chip_peer, 2, core_peer).start()

    def space_keys(frame, t):
        kv_copy(frame, t, core_peer, 0, core_peer).wait_recv()
        for k in range(4):
            src = lax.bitwise_xor(band, k)
            if k == 3:
                kv_copy(frame, t, src, 2, core_peer).wait_recv()
            at = slice(k * ROWS, (k + 1) * ROWS)
            keys_t[frame, t, :, at] = kv_all[frame, t, src, :, 0:128].T
            value_tile = kv_all[frame, t, src, :, 128:256]
            for parity in range(2):
                vals[frame, 2 * t + parity, at, :] = with_ones(value_tile, parity)

    def space_half(frame, half, blocks):
        start = frame * ROWS + half * HALF

        def scores_of(block):
            q = queries[4 * block : 4 * block + 4, start : start + HALF, :].reshape(4 * HALF, 128)
            return jnp.dot(q, keys_t[frame, block // 2], preferred_element_type=F32)

        ahead = scores_of(blocks[0])
        for block in blocks:
            parity = block % 2
            scores, ahead = ahead, (scores_of(block + 1) if block != blocks[-1] else None)
            largest = jnp.max(scores, axis=-1, keepdims=True)
            weights = jnp.exp2((scores - largest) * EXP_SCALE).astype(BF16)
            done = jnp.dot(weights, vals[frame, block], preferred_element_type=F32)
            for k in range(2):
                att[2 * frame + half, 2 * block + k] = join_heads(
                    done[2 * k * HALF : (2 * k + 1) * HALF], done[(2 * k + 1) * HALF : (2 * k + 2) * HALF], parity
                ).astype(BF16)

    def block_columns(left_ref, w_ref, n):
        left = jnp.concatenate([left_ref[k] for k in range(8)], axis=1)
        return jnp.dot(left, w_ref[:, n * 256 : (n + 1) * 256], preferred_element_type=F32)

    def all_of(buf, dst, frame, send_sem, recv_sem, count=PEERS - 1):
        return pltpu.make_async_remote_copy(
            src_ref=buf.at[frame, pl.ds(0, count)], dst_ref=dst.at[frame, pl.ds(0, count)],
            send_sem=send_sem, recv_sem=recv_sem, device_id={"frames": me}, device_id_type=MESH)

    def out_space(frame, half):
        start = frame * ROWS + half * HALF
        for n in range(2):
            packs = []
            for m in (n, n + 2):
                at = slice(m * 256, (m + 1) * 256)
                stream = tok[start : start + HALF, at].astype(F32) + block_columns(att.at[2 * frame + half], wos, m)
                stream = stream.astype(BF16).astype(F32)
                packs.append(pack_rows(stream[:, :128], stream[:, 128:]))
            send_buf[frame, half * 32 : half * 32 + 32, :, n * 128 : (n + 1) * 128] = jnp.concatenate(
                packs, axis=1).astype(BF16)

        def send(k, carry):
            pair = lax.rem(my_pair + k, 32)
            peer = peer_of(pair, half)

            @pl.when(peer != me)
            def _():
                pltpu.make_async_remote_copy(
                    src_ref=send_buf.at[frame, half * 32 + pair], dst_ref=recv_buf.at[frame, me],
                    send_sem=a2a_send.at[frame], recv_sem=a2a_recv.at[frame],
                    device_id={"frames": peer}, device_id_type=MESH).start()

            return carry

        lax.fori_loop(0, 32, send, 0)

        @pl.when(my_half == half)
        def _():
            recv_buf[frame, me] = send_buf[frame, half * 32 + my_pair]

    forward(0, 0)
    space_keys(0, 0)
    space_half(0, 0, (0, 1))
    forward(0, 1)
    space_half(0, 1, (0, 1))
    space_keys(0, 1)
    space_half(0, 0, (2, 3))
    loads["wos"].wait()
    out_space(0, 0)
    forward(1, 0)
    forward(1, 1)
    space_keys(1, 0)
    space_keys(1, 1)
    space_half(1, 0, (0, 1, 2, 3))
    out_space(1, 0)
    space_half(0, 1, (2, 3))
    out_space(0, 1)
    space_half(1, 1, (0, 1, 2, 3))
    out_space(1, 1)

    gain_time = gain_row(nt_ref)
    query_gain_t = pair_gain(qkt_ref, 0)
    key_gain_t = pair_gain(qkt_ref, 1)
    for name in ("wqt", "wkvt", "wot"):
        loads[name].wait()

    def arrive(frame):
        all_of(send_buf, recv_buf, frame, a2a_send.at[frame], a2a_recv.at[frame]).wait_recv()
        for n in range(2):
            pack = recv_buf[frame, :, :, n * 128 : (n + 1) * 128].astype(F32)
            for half, m in enumerate((n, n + 2)):
                left, right = unpack_rows(pack[:, half * 8 : (half + 1) * 8, :])
                shuffle[2 * m] = left
                shuffle[2 * m + 1] = right
        for j in range(POS):
            rows = slice(j * 64, (j + 1) * 64)
            values = jnp.concatenate([shuffle[k, pl.ds(j, 64, stride=4), :] for k in range(8)], axis=1)
            stream_t[frame, rows, :] = values.astype(BF16)
            normed_t[rows, :] = normalise(values, gain_time)
        hidden = normed_t[...]
        part = jnp.dot(hidden, wkvt[...], preferred_element_type=F32)
        for t in range(2):
            key_tile = rms_pair(part[:, t * 128 : (t + 1) * 128], key_gain_t, ones_block)
            value_tile = part[:, 256 + t * 128 : 256 + (t + 1) * 128]
            for kv, key_side, value_side in zip((2 * t, 2 * t + 1), both_sides(key_tile), both_sides(value_tile)):
                for side in range(2):
                    for j in range(POS):
                        rows = slice(j * 64, (j + 1) * 64)
                        keep = slice(side * 128 + frame * 64, side * 128 + frame * 64 + 64)
                        keys_time[j, kv, keep, :] = key_side[side][rows]
                        vals_time[j, kv, keep, 0:128] = value_side[side][rows]
        for n in range(4):
            part = jnp.dot(hidden, wqt[:, n * 256 : (n + 1) * 256], preferred_element_type=F32)
            for k in range(2):
                pair = 2 * n + k
                tile = rms_pair(part[:, k * 128 : (k + 1) * 128], query_gain_t, ones_block).astype(BF16)
                for j in range(POS):
                    queries_t[frame, j, pair] = tile[j * 64 : (j + 1) * 64]

    def time_half(frame):
        q_frame = 2 * (lax.broadcasted_iota(jnp.int32, (128, 128), 0) % 64) + frame
        k_row = lax.broadcasted_iota(jnp.int32, (128, 128), 1)
        allowed = q_frame >= 2 * (k_row % 64) + k_row // 64

        for j in range(POS):
            rows = slice(j * 64, (j + 1) * 64)
            for kv in range(KV_HEADS):
                q = queries_t[frame, j, 2 * kv : 2 * kv + 2].reshape(128, 128)
                scores = lax.dot_general(q, keys_time[j, kv], (((1,), (1,)), ((), ())), preferred_element_type=F32)
                weights = []
                for side in range(2):
                    mine = jnp.where(allowed, scores[:, side * 128 : (side + 1) * 128], -1e30)
                    largest = jnp.max(mine, axis=-1, keepdims=True)
                    weights.append(jnp.exp2((mine - largest) * EXP_SCALE).astype(BF16))
                done = jnp.dot(jnp.concatenate(weights, axis=1), vals_time[j, kv], preferred_element_type=F32)
                out = (done[:, :128] / done[:, 128:]).astype(BF16)
                att_t[2 * kv, rows, :] = out[:64]
                att_t[2 * kv + 1, rows, :] = out[64:]
        for n in range(4):
            at = slice(n * 256, (n + 1) * 256)
            mixed = stream_t[frame, :, at].astype(F32) + block_columns(att_t, wot, n)
            mixed = mixed.astype(BF16).astype(F32)
            for j in range(POS):
                for half in range(2):
                    shuffle[2 * n + half, pl.ds(j, 64, stride=4), :] = mixed[
                        j * 64 : (j + 1) * 64, half * 128 : (half + 1) * 128]
        for n in range(2):
            packs = [pack_rows(shuffle[2 * m], shuffle[2 * m + 1]) for m in (n, n + 2)]
            back_buf[frame, :, :, n * 128 : (n + 1) * 128] = jnp.concatenate(packs, axis=1).astype(BF16)

        def send(k, carry):
            peer = lax.rem(me + k, PEERS)
            pltpu.make_async_remote_copy(
                src_ref=back_buf.at[frame, peer], dst_ref=home_buf.at[frame, my_half * 32 + my_pair],
                send_sem=back_send.at[frame], recv_sem=back_recv.at[frame, my_half],
                device_id={"frames": peer}, device_id_type=MESH).start()
            return carry

        lax.fori_loop(1, PEERS, send, 0)
        home_buf[frame, my_half * 32 + my_pair] = back_buf[frame, me]

    arrive(0)
    arrive(1)
    time_half(0)
    time_half(1)

    def finish(frame, half):
        for count in (31, 32):
            @pl.when(my_half == half if count == 31 else my_half != half)
            def _():
                all_of(back_buf, home_buf, frame, back_send.at[frame], back_recv.at[frame, half], count).wait_recv()

        rows = slice(half * HALF, (half + 1) * HALF)
        for n in range(2):
            pack = home_buf[frame, half * 32 : half * 32 + 32, :, n * 128 : (n + 1) * 128].astype(F32)
            for part, m in enumerate((n, n + 2)):
                left, right = unpack_rows(pack[:, part * 8 : (part + 1) * 8, :])
                out_buf[frame, rows, m * 256 : m * 256 + 128] = left.astype(BF16)
                out_buf[frame, rows, m * 256 + 128 : (m + 1) * 256] = right.astype(BF16)
        copy = pltpu.make_async_copy(out_buf.at[frame, rows], out_hbm.at[frame, rows], out_sem.at[frame, half])
        copy.start()
        return copy

    copies = [finish(0, 0), finish(1, 0), finish(0, 1), finish(1, 1)]
    for frame in range(2):
        for t in range(2):
            kv_copy(frame, t, band, 0, core_peer).wait_send()
            kv_copy(frame, t, band, 1, chip_peer).wait_send()
            kv_copy(frame, t, chip_peer, 2, core_peer).wait_send()
        all_of(send_buf, recv_buf, frame, a2a_send.at[frame], a2a_recv.at[frame]).wait_send()
        all_of(back_buf, home_buf, frame, back_send.at[frame], back_recv.at[frame, 0]).wait_send()
    for copy in copies:
        copy.wait()


def body(tokens, norm_space, query_space, keyval_space, out_space, qk_space,
         norm_time, query_time, keyval_time, out_time, qk_time):
    frames_here, rows_here, width = tokens.shape
    any_spec = pl.BlockSpec(memory_space=pl.ANY)
    vmem = pl.BlockSpec(memory_space=pltpu.VMEM)
    dma = pltpu.SemaphoreType.DMA
    return pl.pallas_call(
        kernel,
        out_shape=jax.ShapeDtypeStruct((frames_here, rows_here, width), BF16),
        in_specs=[any_spec, vmem, any_spec, any_spec, any_spec, vmem, vmem, any_spec, any_spec, any_spec, vmem],
        out_specs=any_spec,
        scratch_shapes=[
            pltpu.VMEM((2 * ROWS, D), BF16),
            pltpu.VMEM((D, D), BF16), pltpu.VMEM((D, 512), BF16), pltpu.VMEM((D, D), BF16),
            pltpu.VMEM((D, D), BF16), pltpu.VMEM((D, 512), BF16), pltpu.VMEM((D, D), BF16),
            pltpu.VMEM((2 * ROWS, D), BF16),
            pltpu.VMEM((HEADS, 2 * ROWS, 128), BF16),
            pltpu.VMEM((2, 2, 4, ROWS, 256), BF16),
            pltpu.VMEM((2, 2, 128, 4 * ROWS), BF16),
            pltpu.VMEM((2, KV_HEADS, 4 * ROWS, 128), BF16),
            pltpu.VMEM((4, 8, HALF, 128), BF16),
            pltpu.VMEM((2, PEERS, 16, 256), BF16),
            pltpu.VMEM((2, PEERS, 16, 256), BF16),
            pltpu.VMEM((8, ROWS, 128), F32),
            pltpu.VMEM((2, ROWS, D), BF16),
            pltpu.VMEM((ROWS, D), BF16),
            pltpu.VMEM((2, POS, HEADS // 2, 64, 128), BF16),
            pltpu.VMEM((POS, KV_HEADS, 256, 128), BF16),
            pltpu.VMEM((POS, KV_HEADS, 256, 256), BF16),
            pltpu.VMEM((8, ROWS, 128), BF16),
            pltpu.VMEM((2, PEERS, 16, 256), BF16),
            pltpu.VMEM((2, PEERS, 16, 256), BF16),
            pltpu.VMEM((2, ROWS, D), BF16),
            dma((7,)), dma((2, 2, 3)), dma((2, 2, 3)), dma((2,)), dma((2,)), dma((2,)), dma((2, 2)), dma((2, 2)),
        ],
        compiler_params=pltpu.CompilerParams(
            collective_id=0, has_side_effects=True, vmem_limit_bytes=58 * 2**20
        ),
        name="block",
    )(
        tokens.reshape(frames_here * rows_here, width), norm_space.reshape(8, 128), query_space, keyval_space,
        out_space, qk_space, norm_time.reshape(8, 128), query_time, keyval_time, out_time, qk_time,
    )


def solution(mesh):
    placed = (P("frames", "band", None), P(), P(), P(), P(), P(), P(), P(), P(), P(), P())
    return jax.shard_map(
        body, mesh=mesh, in_specs=placed, out_specs=P("frames", "band", None), check_vma=False
    )
```

```python
import functools

import jax
import jax.numpy as jnp
from jax import lax
from jax.experimental import pallas as pl
from jax.experimental.pallas import tpu as pltpu
from jax.sharding import PartitionSpec as P

HEADS = 16
KV_HEADS = 4
HEAD_DIM = 64
D = 1024
ROWS = 256
HALF = 128
PEERS = 64
POS = 4
MESH = pl.DeviceIdType.MESH
F32 = jnp.float32
BF16 = jnp.bfloat16
EXP_SCALE = 0.125 * 1.4426950408889634


def lane_half(shape):
    return lax.broadcasted_iota(jnp.int32, shape, len(shape) - 1) // HEAD_DIM


def rms_pair(tile, gain, ones_block):
    squares = tile * tile
    high = squares.astype(BF16)
    low = (squares - high.astype(F32)).astype(BF16)
    mean = jnp.dot(jnp.concatenate([high, low], axis=1), ones_block, preferred_element_type=F32)
    return tile * lax.rsqrt(mean + 1e-06) * gain


def head_queries(tile, pair):
    parity = (pair // 2) % 2
    here = lane_half(tile.shape) == parity
    turned = pltpu.roll(tile, HEAD_DIM, 1)
    first, second = (tile, turned) if parity == 0 else (turned, tile)
    zero = jnp.zeros_like(tile)
    return jnp.where(here, first, zero).astype(BF16), jnp.where(here, second, zero).astype(BF16)


def join_heads(first, second, parity):
    low = lane_half(first.shape) == 0
    if parity == 0:
        turned = pltpu.roll(second, HEAD_DIM, 1)
        over, under = jnp.where(low, first, turned), jnp.where(low, pltpu.roll(first, HEAD_DIM, 1), second)
    else:
        turned = pltpu.roll(first, HEAD_DIM, 1)
        over, under = jnp.where(low, turned, second), jnp.where(low, first, pltpu.roll(second, HEAD_DIM, 1))
    return over / under


def with_ones(tile, parity):
    return jnp.where(lane_half(tile.shape) == parity, tile, jnp.ones_like(tile))


def both_sides(tile):
    low = lane_half(tile.shape) == 0
    turned = pltpu.roll(tile, HEAD_DIM, 1)
    zero = jnp.zeros_like(tile)
    return (
        (jnp.where(low, tile, zero).astype(BF16), jnp.where(low, zero, turned).astype(BF16)),
        (jnp.where(low, turned, zero).astype(BF16), jnp.where(low, zero, tile).astype(BF16)),
    )


def pack_rows(left, right):
    peers = left.shape[0] // POS
    left = left.reshape(peers // 2, 8, 128)
    right = right.reshape(peers // 2, 8, 128)
    low = lax.broadcasted_iota(jnp.int32, left.shape, 1) < 4
    even = jnp.where(low, left, pltpu.roll(right, 4, 1))
    odd = jnp.where(low, pltpu.roll(left, 4, 1), right)
    return jnp.stack([even, odd], axis=1).reshape(peers, 8, 128)


def unpack_rows(packed):
    peers = packed.shape[0]
    packed = packed.reshape(peers // 2, 2, 8, 128)
    even, odd = packed[:, 0], packed[:, 1]
    low = lax.broadcasted_iota(jnp.int32, even.shape, 1) < 4
    left = jnp.where(low, even, pltpu.roll(odd, 4, 1))
    right = jnp.where(low, pltpu.roll(even, 4, 1), odd)
    return left.reshape(peers * POS, 128), right.reshape(peers * POS, 128)


def gain_row(ref):
    return jnp.concatenate([ref[k : k + 1, :] for k in range(8)], axis=1)


def normalise(values, gain):
    return (values * lax.rsqrt(jnp.mean(values * values, axis=-1, keepdims=True) + 1e-06) * gain).astype(BF16)


def kernel(
    tok_hbm, ns_ref, wqs_hbm, wkvs_hbm, wos_hbm, qks_ref, nt_ref, wqt_hbm, wkvt_hbm, wot_hbm, qkt_ref,
    home,
    tok, wqs, wkvs, wos, wqt, wkvt, wot,
    normed, queries, kv_all, keys_t, vals, att, send_buf, recv_buf,
    shuffle, stream_t, normed_t, queries_t, keys_time, vals_time, att_t, back_buf,
    load_sem, kv_send, kv_recv, a2a_send, a2a_recv, back_send, back_recv, own_sem,
):
    me = lax.axis_index("frames")
    band = lax.axis_index("band")
    my_pair = lax.div(me, 2)
    my_half = lax.rem(lax.rem(me, 2) + lax.div(my_pair, 8) + lax.rem(my_pair, 8), 2)

    def peer_of(pair, half):
        return 2 * pair + lax.rem(half + lax.div(pair, 8) + lax.rem(pair, 8), 2)

    core_peer = lax.bitwise_xor(band, 1)
    chip_peer = lax.bitwise_xor(band, 2)

    loads = {}
    for k, (name, src, dst) in enumerate(
        [("tok", tok_hbm, tok), ("wkvs", wkvs_hbm, wkvs), ("wqs", wqs_hbm, wqs), ("wos", wos_hbm, wos),
         ("wqt", wqt_hbm, wqt), ("wkvt", wkvt_hbm, wkvt), ("wot", wot_hbm, wot)]
    ):
        loads[name] = pltpu.make_async_copy(src, dst, load_sem.at[k])
    loads["tok"].start()
    loads["wkvs"].start()

    barrier = pltpu.get_barrier_semaphore()

    def greet(k, carry):
        pl.semaphore_signal(barrier, inc=1, device_id={"frames": lax.rem(me + k, PEERS)}, device_id_type=MESH)
        return carry

    lax.fori_loop(1, PEERS, greet, 0)
    for peer in (core_peer, chip_peer):
        pl.semaphore_signal(barrier, inc=1, device_id={"band": peer}, device_id_type=MESH)

    row = lax.broadcasted_iota(jnp.int32, (256, 128), 0)
    col = lax.broadcasted_iota(jnp.int32, (256, 128), 1)
    ones_block = jnp.where((row // HEAD_DIM) % 2 == col // HEAD_DIM, 1.0 / HEAD_DIM, 0.0).astype(BF16)

    sides = jnp.where(row // 128 == col // HEAD_DIM, 1.0, 0.0).astype(BF16)
    for j in range(POS):
        for kv in range(KV_HEADS):
            vals_time[j, kv, :, 128:256] = sides

    def pair_gain(ref, k):
        return jnp.concatenate([ref[k : k + 1, :], ref[k : k + 1, :]], axis=1)

    loads["tok"].wait()
    gain_space = gain_row(ns_ref)

    for name in ("wqs", "wos", "wqt", "wkvt", "wot"):
        loads[name].start()

    def kv_copy(frame, t, slot, kind, peer):
        return pltpu.make_async_remote_copy(
            src_ref=kv_all.at[frame, t, slot], dst_ref=kv_all.at[frame, t, slot],
            send_sem=kv_send.at[frame, t, kind], recv_sem=kv_recv.at[frame, t, kind],
            device_id={"band": peer}, device_id_type=MESH)

    key_gain = pair_gain(qks_ref, 1)
    for frame in range(2):
        def norm_rows(k, carry):
            rows = pl.ds(pl.multiple_of(frame * ROWS + k * 64, 64), 64)
            normed[rows, :] = normalise(tok[rows, :].astype(F32), gain_space)
            return carry

        lax.fori_loop(0, ROWS // 64, norm_rows, 0)
        if frame == 0:
            loads["wkvs"].wait()
        rows = slice(frame * ROWS, (frame + 1) * ROWS)
        part = jnp.dot(normed[rows, :], wkvs[...], preferred_element_type=F32)
        for t in range(2):
            tile = part[:, t * 128 : (t + 1) * 128]
            kv_all[frame, t, band, :, 0:128] = rms_pair(tile, key_gain, ones_block).astype(BF16)
            kv_all[frame, t, band, :, 128:256] = part[:, 256 + t * 128 : 256 + (t + 1) * 128].astype(BF16)
        if frame == 0:
            pl.semaphore_wait(barrier, PEERS - 1 + 2)
        for t in range(2):
            kv_copy(frame, t, band, 1, chip_peer).start()
            kv_copy(frame, t, band, 0, core_peer).start()

    loads["wqs"].wait()
    query_gain = pair_gain(qks_ref, 0)
    for n in range(4):
        part = jnp.dot(normed[...], wqs[:, n * 256 : (n + 1) * 256], preferred_element_type=F32)
        for k in range(2):
            pair = 2 * n + k
            tile = rms_pair(part[:, k * 128 : (k + 1) * 128], query_gain, ones_block)
            first, second = head_queries(tile, pair)
            queries[2 * pair] = first
            queries[2 * pair + 1] = second

    def forward(frame, t):
        kv_copy(frame, t, chip_peer, 1, chip_peer).wait_recv()
        kv_copy(frame, t, chip_peer, 2, core_peer).start()

    def space_keys(frame, t):
        kv_copy(frame, t, core_peer, 0, core_peer).wait_recv()
        for k in range(4):
            src = lax.bitwise_xor(band, k)
            if k == 3:
                kv_copy(frame, t, src, 2, core_peer).wait_recv()
            at = slice(k * ROWS, (k + 1) * ROWS)
            keys_t[frame, t, :, at] = kv_all[frame, t, src, :, 0:128].T
            value_tile = kv_all[frame, t, src, :, 128:256]
            for parity in range(2):
                vals[frame, 2 * t + parity, at, :] = with_ones(value_tile, parity)

    def space_half(frame, half, blocks):
        start = frame * ROWS + half * HALF

        def scores_of(block):
            q = queries[4 * block : 4 * block + 4, start : start + HALF, :].reshape(4 * HALF, 128)
            return jnp.dot(q, keys_t[frame, block // 2], preferred_element_type=F32)

        ahead = scores_of(blocks[0])
        for block in blocks:
            parity = block % 2
            scores, ahead = ahead, (scores_of(block + 1) if block != blocks[-1] else None)
            largest = jnp.max(scores, axis=-1, keepdims=True)
            weights = jnp.exp2((scores - largest) * EXP_SCALE).astype(BF16)
            done = jnp.dot(weights, vals[frame, block], preferred_element_type=F32)
            for k in range(2):
                att[half, 2 * block + k] = join_heads(
                    done[2 * k * HALF : (2 * k + 1) * HALF], done[(2 * k + 1) * HALF : (2 * k + 2) * HALF], parity
                ).astype(BF16)

    def block_columns(left_ref, w_ref, n):
        left = jnp.concatenate([left_ref[k] for k in range(8)], axis=1)
        return jnp.dot(left, w_ref[:, n * 256 : (n + 1) * 256], preferred_element_type=F32)

    def all_of(buf, dst, frame, send_sem, recv_sem, count=PEERS - 1):
        return pltpu.make_async_remote_copy(
            src_ref=buf.at[frame, pl.ds(0, count)], dst_ref=dst.at[frame, pl.ds(0, count)],
            send_sem=send_sem, recv_sem=recv_sem, device_id={"frames": me}, device_id_type=MESH)

    def out_space(frame, half):
        start = frame * ROWS + half * HALF
        for n in range(2):
            packs = []
            for m in (n, n + 2):
                at = slice(m * 256, (m + 1) * 256)
                stream = tok[start : start + HALF, at].astype(F32) + block_columns(att.at[half], wos, m)
                stream = stream.astype(BF16).astype(F32)
                packs.append(pack_rows(stream[:, :128], stream[:, 128:]))
            send_buf[frame, half * 32 : half * 32 + 32, :, n * 128 : (n + 1) * 128] = jnp.concatenate(
                packs, axis=1).astype(BF16)

        def send(k, carry):
            pair = lax.rem(my_pair + k, 32)
            peer = peer_of(pair, half)

            @pl.when(peer != me)
            def _():
                pltpu.make_async_remote_copy(
                    src_ref=send_buf.at[frame, half * 32 + pair], dst_ref=recv_buf.at[frame, me],
                    send_sem=a2a_send.at[frame], recv_sem=a2a_recv.at[frame],
                    device_id={"frames": peer}, device_id_type=MESH).start()

            return carry

        lax.fori_loop(0, 32, send, 0)

        @pl.when(my_half == half)
        def _():
            recv_buf[frame, me] = send_buf[frame, half * 32 + my_pair]

    forward(0, 0)
    space_keys(0, 0)
    space_half(0, 0, (0, 1))
    forward(0, 1)
    space_half(0, 1, (0, 1))
    space_keys(0, 1)
    space_half(0, 0, (2, 3))
    loads["wos"].wait()
    out_space(0, 0)
    forward(1, 0)
    space_half(0, 1, (2, 3))
    out_space(0, 1)
    forward(1, 1)
    space_keys(1, 0)
    space_keys(1, 1)
    for half in range(2):
        space_half(1, half, (0, 1, 2, 3))
        out_space(1, half)

    gain_time = gain_row(nt_ref)
    query_gain_t = pair_gain(qkt_ref, 0)
    key_gain_t = pair_gain(qkt_ref, 1)
    for name in ("wqt", "wkvt", "wot"):
        loads[name].wait()

    def arrive(frame):
        all_of(send_buf, recv_buf, frame, a2a_send.at[frame], a2a_recv.at[frame]).wait_recv()
        for n in range(2):
            pack = recv_buf[frame, :, :, n * 128 : (n + 1) * 128].astype(F32)
            for half, m in enumerate((n, n + 2)):
                left, right = unpack_rows(pack[:, half * 8 : (half + 1) * 8, :])
                shuffle[2 * m] = left
                shuffle[2 * m + 1] = right
        for j in range(POS):
            rows = slice(j * 64, (j + 1) * 64)
            values = jnp.concatenate([shuffle[k, pl.ds(j, 64, stride=4), :] for k in range(8)], axis=1)
            stream_t[frame, rows, :] = values.astype(BF16)
            normed_t[rows, :] = normalise(values, gain_time)
        hidden = normed_t[...]
        part = jnp.dot(hidden, wkvt[...], preferred_element_type=F32)
        for t in range(2):
            key_tile = rms_pair(part[:, t * 128 : (t + 1) * 128], key_gain_t, ones_block)
            value_tile = part[:, 256 + t * 128 : 256 + (t + 1) * 128]
            for kv, key_side, value_side in zip((2 * t, 2 * t + 1), both_sides(key_tile), both_sides(value_tile)):
                for side in range(2):
                    for j in range(POS):
                        rows = slice(j * 64, (j + 1) * 64)
                        keep = slice(side * 128 + frame * 64, side * 128 + frame * 64 + 64)
                        keys_time[j, kv, keep, :] = key_side[side][rows]
                        vals_time[j, kv, keep, 0:128] = value_side[side][rows]
        for n in range(4):
            part = jnp.dot(hidden, wqt[:, n * 256 : (n + 1) * 256], preferred_element_type=F32)
            for k in range(2):
                pair = 2 * n + k
                tile = rms_pair(part[:, k * 128 : (k + 1) * 128], query_gain_t, ones_block).astype(BF16)
                for j in range(POS):
                    queries_t[frame, j, pair] = tile[j * 64 : (j + 1) * 64]

    def time_half(frame):
        q_frame = 2 * (lax.broadcasted_iota(jnp.int32, (128, 128), 0) % 64) + frame
        k_row = lax.broadcasted_iota(jnp.int32, (128, 128), 1)
        allowed = q_frame >= 2 * (k_row % 64) + k_row // 64

        for j in range(POS):
            rows = slice(j * 64, (j + 1) * 64)
            for kv in range(KV_HEADS):
                q = queries_t[frame, j, 2 * kv : 2 * kv + 2].reshape(128, 128)
                scores = lax.dot_general(q, keys_time[j, kv], (((1,), (1,)), ((), ())), preferred_element_type=F32)
                weights = []
                for side in range(2):
                    mine = jnp.where(allowed, scores[:, side * 128 : (side + 1) * 128], -1e30)
                    largest = jnp.max(mine, axis=-1, keepdims=True)
                    weights.append(jnp.exp2((mine - largest) * EXP_SCALE).astype(BF16))
                done = jnp.dot(jnp.concatenate(weights, axis=1), vals_time[j, kv], preferred_element_type=F32)
                out = (done[:, :128] / done[:, 128:]).astype(BF16)
                att_t[2 * kv, rows, :] = out[:64]
                att_t[2 * kv + 1, rows, :] = out[64:]
        for n in range(4):
            at = slice(n * 256, (n + 1) * 256)
            mixed = stream_t[frame, :, at].astype(F32) + block_columns(att_t, wot, n)
            mixed = mixed.astype(BF16).astype(F32)
            for j in range(POS):
                for half in range(2):
                    shuffle[2 * n + half, pl.ds(j, 64, stride=4), :] = mixed[
                        j * 64 : (j + 1) * 64, half * 128 : (half + 1) * 128]
        for n in range(2):
            packs = [pack_rows(shuffle[2 * m], shuffle[2 * m + 1]) for m in (n, n + 2)]
            back_buf[frame, :, :, n * 128 : (n + 1) * 128] = jnp.concatenate(packs, axis=1).astype(BF16)

        def send(k, carry):
            peer = lax.rem(me + k, PEERS)
            pltpu.make_async_remote_copy(
                src_ref=back_buf.at[frame, peer], dst_ref=home.at[frame, my_half * 32 + my_pair],
                send_sem=back_send.at[frame], recv_sem=back_recv.at[frame],
                device_id={"frames": peer}, device_id_type=MESH).start()
            return carry

        lax.fori_loop(1, PEERS, send, 0)
        own = pltpu.make_async_copy(
            back_buf.at[frame, me], home.at[frame, my_half * 32 + my_pair], own_sem.at[frame])
        own.start()
        return own

    arrive(0)
    arrive(1)
    own = [time_half(0), time_half(1)]

    for frame in range(2):
        for t in range(2):
            kv_copy(frame, t, band, 0, core_peer).wait_send()
            kv_copy(frame, t, band, 1, chip_peer).wait_send()
            kv_copy(frame, t, chip_peer, 2, core_peer).wait_send()
        all_of(send_buf, recv_buf, frame, a2a_send.at[frame], a2a_recv.at[frame]).wait_send()
        all_of(back_buf, home, frame, back_send.at[frame], back_recv.at[frame]).wait()
        own[frame].wait()


def place_kernel(home_ref, out_ref):
    for n in range(2):
        pack = home_ref[0, :, :, n * 128 : (n + 1) * 128].astype(F32)
        for part, m in enumerate((n, n + 2)):
            left, right = unpack_rows(pack[:, part * 8 : (part + 1) * 8, :])
            out_ref[0, :, m * 256 : m * 256 + 128] = left.astype(BF16)
            out_ref[0, :, m * 256 + 128 : (m + 1) * 256] = right.astype(BF16)


def body(tokens, norm_space, query_space, keyval_space, out_space, qk_space,
         norm_time, query_time, keyval_time, out_time, qk_time):
    frames_here, rows_here, width = tokens.shape
    any_spec = pl.BlockSpec(memory_space=pl.ANY)
    vmem = pl.BlockSpec(memory_space=pltpu.VMEM)
    dma = pltpu.SemaphoreType.DMA
    home = pl.pallas_call(
        kernel,
        out_shape=jax.ShapeDtypeStruct((2, PEERS, 16, 256), BF16),
        in_specs=[any_spec, vmem, any_spec, any_spec, any_spec, vmem, vmem, any_spec, any_spec, any_spec, vmem],
        out_specs=any_spec,
        scratch_shapes=[
            pltpu.VMEM((2 * ROWS, D), BF16),
            pltpu.VMEM((D, D), BF16), pltpu.VMEM((D, 512), BF16), pltpu.VMEM((D, D), BF16),
            pltpu.VMEM((D, D), BF16), pltpu.VMEM((D, 512), BF16), pltpu.VMEM((D, D), BF16),
            pltpu.VMEM((2 * ROWS, D), BF16),
            pltpu.VMEM((HEADS, 2 * ROWS, 128), BF16),
            pltpu.VMEM((2, 2, 4, ROWS, 256), BF16),
            pltpu.VMEM((2, 2, 128, 4 * ROWS), BF16),
            pltpu.VMEM((2, KV_HEADS, 4 * ROWS, 128), BF16),
            pltpu.VMEM((2, 8, HALF, 128), BF16),
            pltpu.VMEM((2, PEERS, 16, 256), BF16),
            pltpu.VMEM((2, PEERS, 16, 256), BF16),
            pltpu.VMEM((8, ROWS, 128), F32),
            pltpu.VMEM((2, ROWS, D), BF16),
            pltpu.VMEM((ROWS, D), BF16),
            pltpu.VMEM((2, POS, HEADS // 2, 64, 128), BF16),
            pltpu.VMEM((POS, KV_HEADS, 256, 128), BF16),
            pltpu.VMEM((POS, KV_HEADS, 256, 256), BF16),
            pltpu.VMEM((8, ROWS, 128), BF16),
            pltpu.VMEM((2, PEERS, 16, 256), BF16),
            dma((7,)), dma((2, 2, 3)), dma((2, 2, 3)), dma((2,)), dma((2,)), dma((2,)), dma((2,)), dma((2,)),
        ],
        compiler_params=pltpu.CompilerParams(
            collective_id=0, has_side_effects=True, vmem_limit_bytes=58 * 2**20
        ),
        name="block",
    )(
        tokens.reshape(frames_here * rows_here, width), norm_space.reshape(8, 128), query_space, keyval_space,
        out_space, qk_space, norm_time.reshape(8, 128), query_time, keyval_time, out_time, qk_time,
    )
    return pl.pallas_call(
        place_kernel,
        out_shape=jax.ShapeDtypeStruct((frames_here, rows_here, width), BF16),
        grid=(2, 2),
        in_specs=[pl.BlockSpec((1, 32, 16, 256), lambda f, h: (f, h, 0, 0))],
        out_specs=pl.BlockSpec((1, HALF, D), lambda f, h: (f, h, 0)),
        name="place",
    )(home)


def solution(mesh):
    placed = (P("frames", "band", None), P(), P(), P(), P(), P(), P(), P(), P(), P(), P())
    return jax.shard_map(
        body, mesh=mesh, in_specs=placed, out_specs=P("frames", "band", None), check_vma=False
    )
```
